32 devices in a mesh: dp: 32 (over z, y, x, core).
Axes of the slice: x: 2, y: 2, z: 4, core: 2. Of those that a mesh axis runs over, the one named last changes fastest.
Arguments:
- history: bfloat16 [9, 8192, 2048], P(None, 'dp'), may hold values from -6 to 6
- d_out: bfloat16 [8192, 2048], P('dp'), may hold values from -6 to 6
- group_ids: int32 [32], P('dp'), may hold values from 0 to 7
- group_weight: float32 [8], replicated, may hold values from 0.5 to 2
- attn_in: float32 [2048, 6144], P('dp'), may hold values from -0.22097087 to 0.22097087
- attn_out: float32 [2048, 2048], P('dp'), may hold values from -0.8838835 to 0.8838835
- ffn_up: float32 [2048, 8192], P('dp'), may hold values from -0.22097087 to 0.22097087
- ffn_down: float32 [8192, 2048], P('dp'), may hold values from -0.110485435 to 0.110485435
- mixer_in: float32 [2048, 36], P('dp'), may hold values from -0.22097087 to 0.22097087
- mixer_out: float32 [36, 36], replicated, may hold values from -1 to 1
- norm_gain: float32 [3, 2048], P(None, 'dp'), may hold values from 0.5 to 1.5
- norm_bias: float32 [2, 2048], P(None, 'dp'), may hold values from -1.5 to 1.5
- first_attn_in: float32 [2048, 6144], P('dp'), may hold values from -1.9086836 to 1.9086836
- second_attn_in: float32 [2048, 6144], P('dp'), may hold values from 0.022235554 to 0.088942215
- first_attn_out: float32 [2048, 2048], P('dp'), may hold values from -1.9086836 to 1.9086836
- second_attn_out: float32 [2048, 2048], P('dp'), may hold values from 0.022235554 to 0.088942215
- first_ffn_up: float32 [2048, 8192], P('dp'), may hold values from -1.9086836 to 1.9086836
- second_ffn_up: float32 [2048, 8192], P('dp'), may hold values from 0.022235554 to 0.088942215
- first_ffn_down: float32 [8192, 2048], P('dp'), may hold values from -1.9086836 to 1.9086836
- second_ffn_down: float32 [8192, 2048], P('dp'), may hold values from 0.022235554 to 0.088942215
- first_mixer_in: float32 [2048, 36], P('dp'), may hold values from -86.37716 to 86.37716
- second_mixer_in: float32 [2048, 36], P('dp'), may hold values from 45.538414 to 182.15366
- first_mixer_out: float32 [36, 36], replicated, may hold values from -40 to 40
- second_mixer_out: float32 [36, 36], replicated, may hold values from 45.538414 to 182.15366
- first_norm_gain: float32 [3, 2048], P(None, 'dp'), may hold values from -1.75 to 1.75
- second_norm_gain: float32 [3, 2048], P(None, 'dp'), may hold values from 0.088942215 to 0.35576886
- first_norm_bias: float32 [2, 2048], P(None, 'dp'), may hold values from -1.75 to 1.75
- second_norm_bias: float32 [2, 2048], P(None, 'dp'), may hold values from 0.088942215 to 0.35576886
Outputs:
- out_state: bfloat16 [8192, 2048], P('dp')
- grad_history: bfloat16 [9, 8192, 2048], P(None, 'dp')
- global_norm: float32 [], replicated
- lamb_stats: float32 [6, 3], replicated
- next_attn_in: float32 [2048, 6144], P('dp')
- copy_attn_in: bfloat16 [2048, 6144], P('dp')
- next_first_attn_in: float32 [2048, 6144], P('dp')
- next_second_attn_in: float32 [2048, 6144], P('dp')
- next_attn_out: float32 [2048, 2048], P('dp')
- copy_attn_out: bfloat16 [2048, 2048], P('dp')
- next_first_attn_out: float32 [2048, 2048], P('dp')
- next_second_attn_out: float32 [2048, 2048], P('dp')
- next_ffn_up: float32 [2048, 8192], P('dp')
- copy_ffn_up: bfloat16 [2048, 8192], P('dp')
- next_first_ffn_up: float32 [2048, 8192], P('dp')
- next_second_ffn_up: float32 [2048, 8192], P('dp')
- next_ffn_down: float32 [8192, 2048], P('dp')
- copy_ffn_down: bfloat16 [8192, 2048], P('dp')
- next_first_ffn_down: float32 [8192, 2048], P('dp')
- next_second_ffn_down: float32 [8192, 2048], P('dp')
- next_mixer_in: float32 [2048, 36], P('dp')
- copy_mixer_in: bfloat16 [2048, 36], P('dp')
- next_first_mixer_in: float32 [2048, 36], P('dp')
- next_second_mixer_in: float32 [2048, 36], P('dp')
- next_mixer_out: float32 [36, 36], replicated
- copy_mixer_out: bfloat16 [36, 36], replicated
- next_first_mixer_out: float32 [36, 36], replicated
- next_second_mixer_out: float32 [36, 36], replicated
- next_norm_gain: float32 [3, 2048], P(None, 'dp')
- copy_norm_gain: bfloat16 [3, 2048], P(None, 'dp')
- next_first_norm_gain: float32 [3, 2048], P(None, 'dp')
- next_second_norm_gain: float32 [3, 2048], P(None, 'dp')
- next_norm_bias: float32 [2, 2048], P(None, 'dp')
- copy_norm_bias: bfloat16 [2, 2048], P(None, 'dp')
- next_first_norm_bias: float32 [2, 2048], P(None, 'dp')
- next_second_norm_bias: float32 [2, 2048], P(None, 'dp')
The draws below stay inside these ranges and needn't reach their ends.
All inputs are finite; a program needn't handle non-finite values.
Results may differ from the reference program's by a relative error of at most 0.019.
The reference program's roundings to bfloat16 on the way count: a program that leaves them out, or rounds other values in their place, can miss the bound.
Values may be sent and summed in bfloat16 or wider, within the bound.
No kernel may reach another device: no remote copies, remote signals or barrier semaphores. Data moves between devices by JAX's collectives and lax.ppermute only.
A program may use at most 512 MiB of HBM per device.

```python
import math
import jax
import jax.numpy as jnp
from jax import lax

D = 2048
HEADS = 16
HD = 128
FF = 8192
ROT = 32
MIXH = 36
HIST = 9
STREAMS = 4
GROUPS = 8
SEQ = 256
SEQS = 32
TOKENS = 8192
MIXP = 75024
PARAMS = 50416912


def ramped_moment(key, rows, cols, base):
    position = jnp.arange(rows, dtype=jnp.float32) / max(rows - 1, 1)
    lowest = 0.5
    highest = 2.5
    noise = jnp.clip(jax.random.normal(key, (rows, cols), jnp.float32), -4.0, 4.0)
    factor = lowest * jnp.exp(position * math.log(highest / lowest))
    return noise * (base * factor)[:, None]


def ramped_weight(key, rows, cols, fan_in):
    position = jnp.arange(rows, dtype=jnp.float32) / max(rows - 1, 1)
    lowest = 0.6
    highest = 1.8
    noise = jnp.clip(jax.random.normal(key, (rows, cols), jnp.float32), -4.0, 4.0)
    factor = lowest * jnp.exp(position * math.log(highest / lowest))
    return noise * (factor / math.sqrt(fan_in))[:, None]


def matrix_base():
    return 0.3 * math.sqrt(PARAMS / (PARAMS + D * MIXP))


def draw_attn_in(key, part):
    return ramped_weight(jax.random.fold_in(key, 21), D, 3 * D, D)


def draw_attn_out(key, part):
    return ramped_weight(jax.random.fold_in(key, 22), D, D, D // 16)


def draw_ffn_up(key, part):
    return ramped_weight(jax.random.fold_in(key, 23), D, FF, D)


def draw_ffn_down(key, part):
    return ramped_weight(jax.random.fold_in(key, 24), FF, D, FF)


def draw_mixer_in(key, part):
    return ramped_weight(jax.random.fold_in(key, 25), D, MIXH, D)


def draw_first_attn_in(key, part):
    return ramped_moment(jax.random.fold_in(key, 11), D, 3 * D, matrix_base())


def draw_first_attn_out(key, part):
    return ramped_moment(jax.random.fold_in(key, 12), D, D, matrix_base())


def draw_first_ffn_up(key, part):
    return ramped_moment(jax.random.fold_in(key, 13), D, FF, matrix_base())


def draw_first_ffn_down(key, part):
    return ramped_moment(jax.random.fold_in(key, 14), FF, D, matrix_base())


def draw_first_mixer_in(key, part):
    return ramped_moment(jax.random.fold_in(key, 15), D, MIXH, 0.3 * math.sqrt(D * PARAMS / (PARAMS + D * MIXP)))


def plant(values, stream_key, smallest, largest):
    longest = values.shape.index(max(values.shape))
    spots = []
    for shift in (0, 1):
        where = [jax.random.randint(jax.random.fold_in(stream_key, axis), (), 0, length) for axis, length in enumerate(values.shape)]
        where[longest] = (where[longest] + shift) % values.shape[longest]
        spots.append(tuple(where))
    return values.at[spots[0]].set(smallest).at[spots[1]].set(largest)


def block_levels(key, dims, cuts, smallest, largest):
    factor_of, own = 1.0, jax.random.fold_in(key, 6)
    for dim, shards_of in cuts:
        heights = jnp.exp(jax.random.uniform(jax.random.fold_in(own, dim), (shards_of,), jnp.float32, smallest / len(cuts), largest / len(cuts)))
        factor_of = factor_of * jnp.repeat(heights, dims[dim] // shards_of).reshape([-1 if axis == dim else 1 for axis in range(len(dims))])
    return factor_of


def bell_draw(rng, shape, scale, most, shards=(), held_as=jnp.bfloat16):
    level = block_levels(rng, shape, shards, -0.22, 0.18) if shards else 1.0
    array = jax.random.normal(rng, shape, jnp.float32) * scale * level
    return jnp.minimum(jnp.maximum(array, -most), most).astype(held_as)


def setup_inputs(seed: int = 0) -> dict:
    splits = jax.random.split(jax.random.key(seed), 29)
    return {
        "history": bell_draw(splits[0], (HIST, TOKENS, D), 1.0, 6.0, ((1, 32),)),
        "d_out": bell_draw(splits[1], (TOKENS, D), 1.0, 6.0, ((0, 32),)),
        "group_ids": plant(jax.random.randint(splits[2], (SEQS,), 0, GROUPS), jax.random.fold_in(splits[2], 1), 0, GROUPS - 1).astype(jnp.int32),
        "group_weight": jnp.clip(jnp.exp(jax.random.uniform(splits[3], (GROUPS,), jnp.float32, math.log(0.5), math.log(2.0))), 0.5, 2.0),
        "attn_in": draw_attn_in(jax.random.fold_in(splits[28], 71), 0),
        "attn_out": draw_attn_out(jax.random.fold_in(splits[28], 71), 0),
        "ffn_up": draw_ffn_up(jax.random.fold_in(splits[28], 71), 0),
        "ffn_down": draw_ffn_down(jax.random.fold_in(splits[28], 71), 0),
        "mixer_in": draw_mixer_in(jax.random.fold_in(splits[28], 71), 0),
        "mixer_out": bell_draw(splits[9], (MIXH, STREAMS * HIST), MIXH ** -0.5, 1.0, (), jnp.float32),
        "norm_gain": jnp.clip(1.0 + 0.1 * jax.random.normal(splits[10], (3, D), jnp.float32), 0.5, 1.5),
        "norm_bias": bell_draw(splits[11], (2, D), 0.3, 1.5, ((1, 32),), jnp.float32),
        "first_attn_in": draw_first_attn_in(jax.random.fold_in(splits[28], 71), 0),
        "second_attn_in": jnp.clip(jnp.exp(math.log(0.088942215) - 1.3862944 * jax.random.uniform(splits[13], (D, 3 * D), jnp.float32) ** block_levels(splits[13], (D, 3 * D), ((0, 32),), -0.2, 0.2)), 0.022235554, 0.088942215),
        "first_attn_out": draw_first_attn_out(jax.random.fold_in(splits[28], 71), 0),
        "second_attn_out": jnp.clip(jnp.exp(math.log(0.088942215) - 1.3862944 * jax.random.uniform(splits[15], (D, D), jnp.float32) ** block_levels(splits[15], (D, D), ((0, 32),), -0.2, 0.2)), 0.022235554, 0.088942215),
        "first_ffn_up": draw_first_ffn_up(jax.random.fold_in(splits[28], 71), 0),
        "second_ffn_up": jnp.clip(jnp.exp(math.log(0.088942215) - 1.3862944 * jax.random.uniform(splits[17], (D, FF), jnp.float32) ** block_levels(splits[17], (D, FF), ((0, 32),), -0.2, 0.2)), 0.022235554, 0.088942215),
        "first_ffn_down": draw_first_ffn_down(jax.random.fold_in(splits[28], 71), 0),
        "second_ffn_down": jnp.clip(jnp.exp(math.log(0.088942215) - 1.3862944 * jax.random.uniform(splits[19], (FF, D), jnp.float32) ** block_levels(splits[19], (FF, D), ((0, 32),), -0.2, 0.2)), 0.022235554, 0.088942215),
        "first_mixer_in": draw_first_mixer_in(jax.random.fold_in(splits[28], 71), 0),
        "second_mixer_in": jnp.clip(jnp.exp(math.log(182.15366) - 1.3862944 * jax.random.uniform(splits[21], (D, MIXH), jnp.float32) ** block_levels(splits[21], (D, MIXH), ((0, 32),), -0.2, 0.2)), 45.538414, 182.15366),
        "first_mixer_out": bell_draw(splits[22], (MIXH, STREAMS * HIST), (0.3 * (D * PARAMS / (PARAMS + D * MIXP)) ** 0.5), 40.0, (), jnp.float32),
        "second_mixer_out": jnp.clip(jnp.exp(jax.random.uniform(splits[23], (MIXH, STREAMS * HIST), jnp.float32, math.log(45.538414), math.log(182.15366))), 45.538414, 182.15366),
        "first_norm_gain": bell_draw(splits[24], (3, D), (0.6 * (PARAMS / (PARAMS + D * MIXP)) ** 0.5), 1.75, ((1, 32),), jnp.float32),
        "second_norm_gain": jnp.clip(jnp.exp(math.log(0.35576886) - 1.3862944 * jax.random.uniform(splits[25], (3, D), jnp.float32) ** block_levels(splits[25], (3, D), ((1, 32),), -0.2, 0.2)), 0.088942215, 0.35576886),
        "first_norm_bias": bell_draw(splits[26], (2, D), (0.6 * (PARAMS / (PARAMS + D * MIXP)) ** 0.5), 1.75, ((1, 32),), jnp.float32),
        "second_norm_bias": jnp.clip(jnp.exp(math.log(0.35576886) - 1.3862944 * jax.random.uniform(splits[27], (2, D), jnp.float32) ** block_levels(splits[27], (2, D), ((1, 32),), -0.2, 0.2)), 0.088942215, 0.35576886),
    }


@jax.custom_vjp
def low(v):
    return lax.optimization_barrier(v.astype(jnp.bfloat16)).astype(jnp.float32)

@jax.custom_vjp
def low_back(v):
    return v

def low_keep(v):
    return (low(v), None)

def low_pass(kept, grad):
    return (grad,)

def back_keep(v):
    return (v, None)

def back_low(kept, grad):
    return (low(grad),)
low.defvjp(low_keep, low_pass)
low_back.defvjp(back_keep, back_low)
EPS_NORM = 1e-05
EPS_ADAM = 1e-06
DECAY_WEIGHT = 0.01
RATE_MATRIX = 0.3
RATE_VECTOR = 0.25
BETA = 0.5
NEGATIVE = -1e+30
HIGHEST = lax.Precision.HIGHEST

def matmul(left, right):
    return jnp.dot(left, right, preferred_element_type=jnp.float32, precision=HIGHEST)

def layer_norm(values):
    centre = lax.optimization_barrier(jnp.mean(values, axis=-1, keepdims=True))
    centred = values - centre
    spread = lax.optimization_barrier(jnp.mean(centred * centred, axis=-1, keepdims=True))
    return centred * lax.rsqrt(spread + EPS_NORM)

def rotate(values, cosine, sine_table, turn_sign):
    half_width = cosine.shape[-1]
    first_half = values[..., :half_width]
    second = values[..., half_width:2 * half_width]
    return jnp.concatenate([first_half * cosine - turn_sign * second * sine_table, second * cosine + turn_sign * first_half * sine_table, values[..., 2 * half_width:]], axis=-1)

def phases(seq_len):
    half_width = ROT // 2
    frequency = 10000.0 ** (-(2.0 * jnp.arange(half_width, dtype=jnp.float32)) / ROT)
    phase_grid = jnp.arange(seq_len, dtype=jnp.float32)[:, None] * frequency[None, :]
    return (jnp.cos(phase_grid)[:, None, :], jnp.sin(phase_grid)[:, None, :])

def gelu_exact(values):
    return jax.nn.gelu(values, approximate=False)

def forward(attn_in, attn_out, ffn_up, ffn_down, mixer_in, mixer_out, norm_gain, norm_bias, history):
    w_attn_in = low(attn_in)
    w_attn_out = low(attn_out)
    w_ffn_up = low(ffn_up)
    w_ffn_down = low(ffn_down)
    w_mixer_in = low(mixer_in)
    w_mixer_out = low(mixer_out)
    gain_table = low(norm_gain)
    bias_table = low(norm_bias)
    cosine, sine_table = phases(SEQ)
    scale = 1.0 / math.sqrt(HD)
    positions = jnp.arange(SEQ)
    allowed = positions[:, None] >= positions[None, :]

    def one_sequence(sequence):
        mix_normed = low(layer_norm(sequence[HIST - 1]) * gain_table[0])
        mix_pre = low_back(matmul(mix_normed, w_mixer_in))
        mix_hidden = low(gelu_exact(mix_pre))
        coef = low_back(matmul(mix_hidden, w_mixer_out)).reshape(SEQ, STREAMS, HIST)
        streams = jnp.einsum('saj,jsd->asd', coef, sequence, precision=HIGHEST)
        normed = low(layer_norm(streams[:3]) * gain_table[1] + bias_table[0])
        query = low_back(matmul(normed[0], w_attn_in[:, :D])).reshape(SEQ, HEADS, HD)
        keys = low_back(matmul(normed[1], w_attn_in[:, D:2 * D])).reshape(SEQ, HEADS, HD)
        value = low(low_back(matmul(normed[2], w_attn_in[:, 2 * D:]))).reshape(SEQ, HEADS, HD)
        query_rot = low(rotate(query, cosine, sine_table, 1.0))
        key_rot = low(rotate(keys, cosine, sine_table, 1.0))
        raw = jnp.einsum('qhd,khd->hqk', query_rot, key_rot, precision=HIGHEST) * scale
        scores = low_back(jnp.where(allowed[None], raw, NEGATIVE))
        row_max = lax.optimization_barrier(jnp.max(scores, axis=-1, keepdims=True))
        exponent = jnp.exp(scores - row_max)
        probs = exponent / lax.optimization_barrier(jnp.sum(exponent, axis=-1, keepdims=True))
        attended = jnp.einsum('hqk,khd->qhd', low(probs), value, precision=HIGHEST)
        attended = low(low_back(attended.reshape(SEQ, D)))
        residual = low_back(streams[3] + matmul(attended, w_attn_out))
        ffn_normed = low(layer_norm(residual) * gain_table[2] + bias_table[1])
        up_proj = low_back(matmul(ffn_normed, w_ffn_up))
        activated = low(gelu_exact(up_proj))
        return low_back(residual + matmul(activated, w_ffn_down))
    by_sequence = history.reshape(HIST, SEQS, SEQ, D).transpose(1, 0, 2, 3)
    outputs = lax.map(jax.checkpoint(one_sequence), by_sequence)
    return outputs.reshape(TOKENS, D)

def reference(history, d_out, group_ids, group_weight, attn_in, attn_out, ffn_up, ffn_down, mixer_in, mixer_out, norm_gain, norm_bias, first_attn_in, second_attn_in, first_attn_out, second_attn_out, first_ffn_up, second_ffn_up, first_ffn_down, second_ffn_down, first_mixer_in, second_mixer_in, first_mixer_out, second_mixer_out, first_norm_gain, second_norm_gain, first_norm_bias, second_norm_bias):
    weights = (attn_in, attn_out, ffn_up, ffn_down, mixer_in, mixer_out, norm_gain, norm_bias)
    firsts = (first_attn_in, first_attn_out, first_ffn_up, first_ffn_down, first_mixer_in, first_mixer_out, first_norm_gain, first_norm_bias)
    seconds = (second_attn_in, second_attn_out, second_ffn_up, second_ffn_down, second_mixer_in, second_mixer_out, second_norm_gain, second_norm_bias)
    result, pullback = jax.vjp(forward, *weights, history.astype(jnp.float32))
    match_table = jnp.arange(GROUPS, dtype=jnp.int32)[None, :] == group_ids[:, None]
    seq_weight = lax.optimization_barrier(jnp.sum(jnp.where(match_table, group_weight[None, :], 0.0), axis=1))
    row_weight = jnp.repeat(seq_weight, SEQ)
    cotangent = d_out.astype(jnp.float32) * row_weight[:, None]
    gradients = pullback(cotangent)
    grads = gradients[:8]
    grad_hist = gradients[8]
    squares = sum((jnp.sum(grad_item * grad_item) for grad_item in grads))
    global_norm = jnp.sqrt(squares)
    clip = 0.3 * math.sqrt(PARAMS) / (global_norm + 1e-06)
    results = []
    stat_rows = []
    for member in range(8):
        scaled = grads[member] * clip
        first_new = BETA * firsts[member] + (1.0 - BETA) * scaled
        second_new = BETA * seconds[member] + (1.0 - BETA) * scaled * scaled
        step_value = first_new / (jnp.sqrt(second_new) + EPS_ADAM)
        weight_now = weights[member]
        if member < 6:
            step_value = step_value + DECAY_WEIGHT * weight_now
            weight_norm = jnp.sqrt(jnp.sum(weight_now * weight_now))
            update_norm = jnp.sqrt(jnp.sum(step_value * step_value))
            trust = weight_norm / (update_norm + 1e-06)
            stat_rows.append(jnp.stack([weight_norm, update_norm, trust]))
            updated = weight_now - RATE_MATRIX * trust * step_value
        else:
            updated = weight_now - RATE_VECTOR * step_value
        results.append((updated, updated.astype(jnp.bfloat16), first_new, second_new))
    lamb_stats = jnp.stack(stat_rows)
    return (result.astype(jnp.bfloat16), grad_hist.astype(jnp.bfloat16), global_norm, lamb_stats, results[0][0], results[0][1], results[0][2], results[0][3], results[1][0], results[1][1], results[1][2], results[1][3], results[2][0], results[2][1], results[2][2], results[2][3], results[3][0], results[3][1], results[3][2], results[3][3], results[4][0], results[4][1], results[4][2], results[4][3], results[5][0], results[5][1], results[5][2], results[5][3], results[6][0], results[6][1], results[6][2], results[6][3], results[7][0], results[7][1], results[7][2], results[7][3])
```

```python
import functools
import math

import jax
import jax.numpy as jnp
from jax import lax
from jax.experimental import pallas as pl
from jax.experimental.pallas import tpu as pltpu
from jax.sharding import PartitionSpec as P

HD = 128
ROT = 32
PARAMS = 50416912

EPS_NORM = 1e-05
EPS_ADAM = 1e-06
DECAY_WEIGHT = 0.01
RATE_MATRIX = 0.3
RATE_VECTOR = 0.25
BETA = 0.5
NEGATIVE = -1e30

BF = jnp.bfloat16
F32 = jnp.float32


def layer_norm(values):
    centre = jnp.mean(values, axis=-1, keepdims=True)
    centred = values - centre
    spread = jnp.mean(centred * centred, axis=-1, keepdims=True)
    return centred * lax.rsqrt(spread + EPS_NORM)


def scaled_norm(values, gain_row):
    return layer_norm(values) * gain_row


def shifted_norm(values, gain_row, shift_row):
    return layer_norm(values) * gain_row + shift_row


def gelu_exact(values):
    return jax.nn.gelu(values, approximate=False)


def dot(left, right):
    return jnp.dot(left, right, preferred_element_type=F32)


def dot_tn(left, right):
    return lax.dot_general(left, right, (((0,), (0,)), ((), ())), preferred_element_type=F32)


def dot_nt(left, right):
    return lax.dot_general(left, right, (((1,), (1,)), ((), ())), preferred_element_type=F32)


def mix_history(coef, history):
    total_mix = jnp.zeros((coef.shape[1],) + history.shape[1:], F32)
    for member in range(history.shape[0]):
        total_mix = (
            total_mix
            + jnp.transpose(coef[:, :, member])[:, :, None] * history[member].astype(F32)[None]
        )
    return total_mix


def rotary_tables(seq_len):
    half_width = ROT // 2
    frequency = 10000.0 ** (-(2.0 * jnp.arange(half_width, dtype=F32)) / ROT)
    angles = jnp.arange(seq_len, dtype=F32)[:, None] * frequency[None, :]
    cosine, sine = jnp.cos(angles), jnp.sin(angles)
    rest = HD - ROT
    cos_table = jnp.concatenate([cosine, cosine, jnp.ones((seq_len, rest), F32)], axis=1)
    sin_table = jnp.concatenate([-sine, sine, jnp.zeros((seq_len, rest), F32)], axis=1)
    return cos_table, sin_table


def turn(values, cos_table, sin_table):
    half_width = ROT // 2
    lane = lax.broadcasted_iota(jnp.int32, values.shape, 1)
    partner = jnp.where(
        lane < half_width,
        pltpu.roll(values, HD - half_width, axis=1),
        pltpu.roll(values, half_width, axis=1),
    )
    return values * cos_table + partner * sin_table


def head_scores(query, key):
    seq_len = query.shape[0]
    scores = dot_nt(query, key) * (1.0 / math.sqrt(HD))
    row = lax.broadcasted_iota(jnp.int32, (seq_len, seq_len), 0)
    column = lax.broadcasted_iota(jnp.int32, (seq_len, seq_len), 1)
    scores = jnp.where(row >= column, scores, NEGATIVE)
    exponent = jnp.exp(scores - jnp.max(scores, axis=-1, keepdims=True))
    return exponent / jnp.sum(exponent, axis=-1, keepdims=True)


def attention_forward_kernel(q_ref, k_ref, v_ref, cos_ref, sin_ref, o_ref, qr_ref, kr_ref):
    cos_table, sin_table = cos_ref[...], sin_ref[...]
    query = turn(q_ref[...], cos_table, sin_table).astype(BF)
    key = turn(k_ref[...], cos_table, sin_table).astype(BF)
    qr_ref[...] = query
    kr_ref[...] = key
    probs = head_scores(query, key).astype(BF)
    o_ref[...] = dot(probs, v_ref[...]).astype(BF)


def attention_backward_kernel(
    q_ref, k_ref, v_ref, g_ref, cos_ref, sin_ref, dq_ref, dk_ref, dv_ref
):
    scale = 1.0 / math.sqrt(HD)
    cos_table, sin_table = cos_ref[...], -sin_ref[...]
    query, key, grad = q_ref[...], k_ref[...], g_ref[...]
    probs = head_scores(query, key)
    grad_probs = dot_nt(grad, v_ref[...])
    centre = jnp.sum(probs * grad_probs, axis=-1, keepdims=True)
    grad_scores = (probs * (grad_probs - centre)).astype(BF)
    dq_ref[...] = turn(dot(grad_scores, key) * scale, cos_table, sin_table).astype(BF)
    dk_ref[...] = turn(dot_tn(grad_scores, query) * scale, cos_table, sin_table).astype(BF)
    dv_ref[...] = dot_tn(probs.astype(BF), grad).astype(BF)


def attention_call(kernel, seq_len, blocks, tables, out_types):
    rows, width = blocks[0].shape
    head_block = pl.BlockSpec((seq_len, HD), lambda s, h: (s, h))
    table_block = pl.BlockSpec((seq_len, HD), lambda s, h: (0, 0))
    return pl.pallas_call(
        kernel,
        grid=(rows // seq_len, width // HD),
        in_specs=[head_block] * len(blocks) + [table_block] * 2,
        out_specs=[head_block] * len(out_types),
        out_shape=[jax.ShapeDtypeStruct((rows, width), kind) for kind in out_types],
        compiler_params=pltpu.CompilerParams(vmem_limit_bytes=32 * 1024 * 1024),
        cost_estimate=pl.CostEstimate(
            flops=rows * width * seq_len * 10,
            bytes_accessed=rows * width * 16,
            transcendentals=rows * width * seq_len // HD,
        ),
    )(*blocks, *tables)


class Links:
    def __init__(self, devices):
        self.devices = devices
        self.planes = devices // 8
        index = lax.axis_index("dp")
        self.index = index
        self.core = index & 1
        self.x = (index >> 1) & 1
        self.y = (index >> 2) & 1
        self.z = index >> 3
        self.rank = index & 3

    def swap(self, value, bit):
        return lax.ppermute(value, "dp", [(j, j ^ bit) for j in range(self.devices)])

    def swap_core(self, value):
        return self.swap(value, 1)

    def swap_x(self, value):
        return self.swap(value, 2)

    def swap_y(self, value):
        return self.swap(value, 4)

    def z_groups(self):
        return [[j + 8 * k for k in range(self.planes)] for j in range(8)]

    def z_gather(self, value):
        return lax.all_gather(value, "dp", axis=0, tiled=True, axis_index_groups=self.z_groups())

    def z_reduce(self, value):
        return lax.psum_scatter(
            value, "dp", scatter_dimension=0, tiled=True, axis_index_groups=self.z_groups()
        )

    def total(self, value):
        bit = 1
        while bit < self.devices:
            value = value + self.swap(value, bit)
            bit *= 2
        return value


    def to_absolute(self, parts):
        own, across_x, across_core, across_both = parts
        low_x = self.x == 0
        core_own = (jnp.where(low_x, own, across_x), jnp.where(low_x, across_x, own))
        core_other = (
            jnp.where(low_x, across_core, across_both),
            jnp.where(low_x, across_both, across_core),
        )
        low_core = self.core == 0
        ordered = []
        for mine, other in zip(core_own, core_other):
            ordered.append(jnp.where(low_core, mine, other))
            ordered.append(jnp.where(low_core, other, mine))
        return ordered

    def to_relative(self, parts):
        low_x, low_core = self.x == 0, self.core == 0
        near = [jnp.where(low_x, parts[c], parts[2 + c]) for c in (0, 1)]
        far = [jnp.where(low_x, parts[2 + c], parts[c]) for c in (0, 1)]
        return [
            jnp.where(low_core, near[0], near[1]),
            jnp.where(low_core, far[0], far[1]),
            jnp.where(low_core, near[1], near[0]),
            jnp.where(low_core, far[1], far[0]),
        ]

    def group_gather(self, value):
        across_x = self.swap_x(value)
        across = self.swap_core(jnp.stack([value, across_x]))
        return [value, across_x, across[0], across[1]]

    def group_exchange(self, parts):
        own, for_x, for_core, for_both = parts
        from_x = self.swap_x(jnp.stack([for_x, for_both]))
        from_core = self.swap_core(jnp.stack([for_core, from_x[1]]))
        return [own, from_x[0], from_core[0], from_core[1]]

    def group_reduce(self, parts, kind=BF):
        own, for_x, for_core, for_both = parts
        low = lambda part: part.astype(kind)
        from_core = self.swap_core(jnp.stack([low(for_core), low(for_both)]))
        own = own.astype(F32) + from_core[0].astype(F32)
        for_x = for_x.astype(F32) + from_core[1].astype(F32)
        return own + self.swap_x(low(for_x)).astype(F32)

    def split_y(self, values, axis=-1):
        width = values.shape[-1]
        block = width // (2 * self.planes)
        shape = values.shape[:-1]
        halves = jnp.moveaxis(values.reshape(shape + (self.planes, 2, block)), -2, 0)
        halves = halves.reshape((2,) + shape + (width // 2,))
        low_y = self.y == 0
        return jnp.where(low_y, halves[0], halves[1]), jnp.where(low_y, halves[1], halves[0])

    def join_y(self, own, other):
        width = 2 * own.shape[-1]
        block = width // (2 * self.planes)
        shape = own.shape[:-1]
        low_y = self.y == 0
        first = jnp.where(low_y, own, other).reshape(shape + (self.planes, 1, block))
        second = jnp.where(low_y, other, own).reshape(shape + (self.planes, 1, block))
        return jnp.concatenate([first, second], axis=-2).reshape(shape + (width,))


def program(
    devices,
    history,
    d_out,
    group_ids,
    group_weight,
    attn_in,
    attn_out,
    ffn_up,
    ffn_down,
    mixer_in,
    mixer_out,
    norm_gain,
    norm_bias,
    first_attn_in,
    second_attn_in,
    first_attn_out,
    second_attn_out,
    first_ffn_up,
    second_ffn_up,
    first_ffn_down,
    second_ffn_down,
    first_mixer_in,
    second_mixer_in,
    first_mixer_out,
    second_mixer_out,
    first_norm_gain,
    second_norm_gain,
    first_norm_bias,
    second_norm_bias,
):
    links = Links(devices)
    planes = links.planes
    hist_len, seq_len, width = history.shape
    quarter = width // 4
    rows = width // devices
    hidden = ffn_down.shape[0] * devices
    units = hidden // devices

    low_attn = attn_in.astype(BF).reshape(rows, 3, 4, quarter)
    low_out = attn_out.astype(BF).reshape(rows, 1, 4, quarter)
    by_rank = jnp.concatenate([low_attn, low_out], axis=1)
    by_rank = [by_rank[:, :, r].reshape(rows, width) for r in range(4)]
    attn_block = jnp.concatenate(
        links.to_absolute(links.group_exchange(links.to_relative(by_rank))), axis=0
    )

    low_up = ffn_up.astype(BF).reshape(rows, planes * 2, 4, units)
    by_rank = [low_up[:, :, r].reshape(rows, hidden // 4) for r in range(4)]
    up_block = jnp.concatenate(
        links.to_absolute(links.group_exchange(links.to_relative(by_rank))), axis=0
    )
    low_down = ffn_down.astype(BF)
    other_down = links.swap_y(low_down)
    low_y = links.y == 0
    down_block = jnp.concatenate(
        [jnp.where(low_y, low_down, other_down), jnp.where(low_y, other_down, low_down)], axis=0
    )

    attn_own = links.z_gather(attn_block)
    attn_other = links.swap_y(attn_own)
    up_own = links.z_gather(up_block)
    up_other = links.swap_y(up_own)
    w_down = links.z_gather(down_block)

    out_quarter = jnp.concatenate([attn_own[:, 3 * quarter :], attn_other[:, 3 * quarter :]])
    w_out = links.group_gather(out_quarter)

    hidden_mix = mixer_in.shape[1]
    pack = jnp.concatenate([mixer_in.T, norm_gain, norm_bias], axis=0).astype(BF)
    for bit, high in ((1, links.core), (2, links.x), (4, links.y)):
        other = links.swap(pack, bit)
        pack = jnp.concatenate(
            [jnp.where(high == 0, pack, other), jnp.where(high == 0, other, pack)], axis=1
        )
    pieces = [pack]
    for shift in range(1, planes):
        pieces.append(
            lax.ppermute(pack, "dp", [(j, (j + 8 * shift) % devices) for j in range(devices)])
        )
    backwards = jnp.stack([pieces[-k % planes] for k in range(planes)] * 2)
    ordered = lax.dynamic_slice_in_dim(backwards, planes - links.z, planes, axis=0)
    pack = jnp.transpose(ordered, (1, 0, 2)).reshape(pack.shape[0], width)
    w_mixer_in = pack[:hidden_mix]
    gain_table = pack[hidden_mix : hidden_mix + 3].astype(F32)
    bias_table = pack[hidden_mix + 3 :].astype(F32)
    mixer_low = mixer_out.astype(BF)

    current = history[hist_len - 1].astype(F32)
    mix_normed = scaled_norm(current, gain_table[0]).astype(BF)
    mix_pre = dot_nt(mix_normed, w_mixer_in)
    mix_hidden = gelu_exact(mix_pre).astype(BF)
    coef = dot(mix_hidden, mixer_low).reshape(seq_len, -1, hist_len)
    streams = mix_history(coef, history)
    normed = shifted_norm(streams[:3], gain_table[1], bias_table[0]).astype(BF)

    tables = rotary_tables(seq_len)
    normed_own, normed_other, projected = [], [], []
    for a in range(3):
        gathered = jnp.concatenate(links.group_gather(normed[a]), axis=0)
        own, other = links.split_y(gathered)
        normed_own.append(own)
        normed_other.append(other)
        columns = slice(a * quarter, (a + 1) * quarter)
        projected.append(dot(own, attn_own[:, columns]) + dot(other, attn_other[:, columns]))
    value = projected[2].astype(BF)
    attended, query_rot, key_rot = attention_call(
        attention_forward_kernel,
        seq_len,
        (projected[0], projected[1], value),
        tables,
        (BF, BF, BF),
    )
    attended = links.group_exchange(list(attended.reshape(4, seq_len, quarter)))
    attended = jnp.concatenate(links.to_absolute(attended), axis=-1)
    attended = jnp.concatenate(links.split_y(attended), axis=-1)
    out_parts = [dot(attended, part) for part in w_out]
    residual = streams[3] + jnp.concatenate(links.to_absolute(out_parts), axis=-1)

    ffn_normed = shifted_norm(residual, gain_table[2], bias_table[1]).astype(BF)
    gathered = jnp.concatenate(links.group_gather(ffn_normed), axis=0)
    ffn_own, ffn_other = links.split_y(gathered)
    up_proj = dot(ffn_own, up_own) + dot(ffn_other, up_other)
    activated = gelu_exact(up_proj).astype(BF)
    down_parts = dot(activated, w_down).astype(BF).reshape(4, seq_len, width)
    out_state = (residual + links.group_reduce(list(down_parts))).astype(BF)

    group_count = group_weight.shape[0]
    seq_weight = jnp.sum(
        jnp.where(jnp.arange(group_count, dtype=jnp.int32) == group_ids[0], group_weight, 0.0)
    )
    grad_out = (d_out.astype(F32) * seq_weight).astype(BF)
    grad_out_four = jnp.concatenate(links.group_gather(grad_out), axis=0)

    grad_down = dot_tn(activated, grad_out_four).astype(BF)
    grad_down = links.z_reduce(grad_down).reshape(2, units, width)
    down_mine = jnp.where(low_y, grad_down[0], grad_down[1])
    down_theirs = jnp.where(low_y, grad_down[1], grad_down[0])
    shard_down = down_mine.astype(F32) + links.swap_y(down_theirs).astype(F32)

    grad_activated = dot_nt(grad_out_four, w_down)
    _, gelu_back = jax.vjp(gelu_exact, up_proj)
    grad_up = gelu_back(grad_activated)[0].astype(BF)

    def reduce_rows(own, other):
        both = own.astype(F32) + links.swap_y(other.astype(BF)).astype(F32)
        block = links.z_reduce(both.astype(BF))
        parts = list(block.reshape(4, rows, block.shape[1]))
        parts = links.to_absolute(links.group_exchange(links.to_relative(parts)))
        return jnp.stack(parts, axis=1).astype(F32)

    grad_ffn_up = reduce_rows(
        dot_tn(ffn_own, grad_up).astype(BF), dot_tn(ffn_other, grad_up).astype(BF)
    )
    shard_up = jnp.transpose(
        grad_ffn_up.reshape(rows, 4, planes * 2, units), (0, 2, 1, 3)
    ).reshape(rows, hidden)

    back_own = dot_nt(grad_up, up_own).astype(BF).reshape(4, seq_len, width // 2)
    back_other = dot_nt(grad_up, up_other).astype(BF).reshape(4, seq_len, width // 2)
    both = jnp.stack([back_own, back_other], axis=1)
    grad_ffn_normed = links.group_reduce(list(both))
    grad_ffn_normed = links.join_y(grad_ffn_normed[0], grad_ffn_normed[1])
    _, ffn_norm_back = jax.vjp(shifted_norm, residual, gain_table[2], bias_table[1])
    grad_ffn_x, grad_gain_ffn, grad_bias_ffn = ffn_norm_back(grad_ffn_normed)
    grad_residual = (grad_out.astype(F32) + grad_ffn_x).astype(BF)

    residual_parts = links.to_relative(
        [grad_residual[:, r * quarter : (r + 1) * quarter] for r in range(4)]
    )
    grad_attended = dot_nt(residual_parts[0], w_out[0])
    for part, weight in zip(residual_parts[1:], w_out[1:]):
        grad_attended = grad_attended + dot_nt(part, weight)
    grad_attended = grad_attended.astype(BF)
    grad_heads = links.join_y(grad_attended[:, : width // 2], grad_attended[:, width // 2 :])
    grad_heads = links.group_exchange(
        links.to_relative([grad_heads[:, r * quarter : (r + 1) * quarter] for r in range(4)])
    )
    grad_heads = jnp.concatenate(grad_heads, axis=0)
    grad_proj = attention_call(
        attention_backward_kernel,
        seq_len,
        (query_rot, key_rot, value, grad_heads),
        tables,
        (BF, BF, BF),
    )

    out_grads = [dot_tn(attended, part).astype(BF) for part in residual_parts]
    out_grad = links.group_reduce(out_grads)
    grad_attn_out = reduce_rows(out_grad[: width // 2], out_grad[width // 2 :])
    shard_out = grad_attn_out.reshape(rows, width)

    in_own = [dot_tn(normed_own[a], grad_proj[a]).astype(BF) for a in range(3)]
    in_other = [dot_tn(normed_other[a], grad_proj[a]).astype(BF) for a in range(3)]
    grad_attn_in = reduce_rows(jnp.concatenate(in_own, axis=1), jnp.concatenate(in_other, axis=1))
    shard_in = jnp.transpose(
        grad_attn_in.reshape(rows, 4, 3, quarter), (0, 2, 1, 3)
    ).reshape(rows, 3 * width)

    grad_normed = []
    for a in range(3):
        columns = slice(a * quarter, (a + 1) * quarter)
        back_own = dot_nt(grad_proj[a], attn_own[:, columns]).astype(BF)
        back_other = dot_nt(grad_proj[a], attn_other[:, columns]).astype(BF)
        both = jnp.stack(
            [
                back_own.reshape(4, seq_len, width // 2),
                back_other.reshape(4, seq_len, width // 2),
            ],
            axis=1,
        )
        both = links.group_reduce(list(both))
        grad_normed.append(links.join_y(both[0], both[1]))
    grad_normed = jnp.stack(grad_normed)
    _, attn_norm_back = jax.vjp(shifted_norm, streams[:3], gain_table[1], bias_table[0])
    grad_streams, grad_gain_attn, grad_bias_attn = attn_norm_back(grad_normed)

    grad_mixed = jnp.concatenate([grad_streams, grad_residual.astype(F32)[None]], axis=0)
    coef_columns = []
    hist_grads = []
    for member in range(hist_len):
        history_rows = history[member].astype(F32)
        coef_columns.append(jnp.sum(grad_mixed * history_rows[None], axis=-1))
        hist_grads.append(
            jnp.sum(jnp.transpose(coef[:, :, member])[:, :, None] * grad_mixed, axis=0)
        )
    grad_coef = (
        jnp.transpose(jnp.stack(coef_columns, axis=-1), (1, 0, 2)).reshape(seq_len, -1).astype(BF)
    )
    grad_mixer_out = dot_tn(mix_hidden, grad_coef)
    grad_mix_hidden = dot_nt(grad_coef, mixer_low)
    _, mix_gelu_back = jax.vjp(gelu_exact, mix_pre)
    grad_mix_pre = mix_gelu_back(grad_mix_hidden)[0].astype(BF)
    grad_mixer_in = dot_tn(grad_mix_pre, mix_normed)
    grad_mix_normed = dot(grad_mix_pre, w_mixer_in)
    _, mix_norm_back = jax.vjp(scaled_norm, current, gain_table[0])
    grad_current, grad_gain_mix = mix_norm_back(grad_mix_normed)
    hist_grads[hist_len - 1] = hist_grads[hist_len - 1] + grad_current
    grad_history = jnp.stack(hist_grads).astype(BF)

    small = jnp.concatenate(
        [
            grad_mixer_in,
            grad_gain_mix[None],
            grad_gain_attn[None],
            grad_gain_ffn[None],
            grad_bias_attn[None],
            grad_bias_ffn[None],
        ],
        axis=0,
    )
    small = small + links.swap_core(small)
    small = small + links.swap_x(small)
    small_own, small_other = links.split_y(small)
    small = small_own + links.swap_y(small_other)
    blocks = small.reshape(small.shape[0], planes, 4 * rows)
    small = lax.dynamic_index_in_dim(blocks, links.z, axis=1, keepdims=False)
    for shift in range(1, planes):
        sent = lax.dynamic_index_in_dim(
            blocks, (links.z + shift) % planes, axis=1, keepdims=False
        )
        small = small + lax.ppermute(
            sent, "dp", [(j, (j + 8 * shift) % devices) for j in range(devices)]
        )
    small = lax.dynamic_slice_in_dim(small, links.rank * rows, rows, axis=1)
    mixer_grad = links.total(grad_mixer_out)
    grads = (
        shard_in,
        shard_out,
        shard_up,
        shard_down,
        small[:hidden_mix].T,
        mixer_grad,
        small[hidden_mix : hidden_mix + 3],
        small[hidden_mix + 3 :],
    )

    weights = (attn_in, attn_out, ffn_up, ffn_down, mixer_in, mixer_out, norm_gain, norm_bias)
    firsts = (
        first_attn_in,
        first_attn_out,
        first_ffn_up,
        first_ffn_down,
        first_mixer_in,
        first_mixer_out,
        first_norm_gain,
        first_norm_bias,
    )
    seconds = (
        second_attn_in,
        second_attn_out,
        second_ffn_up,
        second_ffn_down,
        second_mixer_in,
        second_mixer_out,
        second_norm_gain,
        second_norm_bias,
    )

    def portion(member, amount):
        return amount / devices if member == 5 else amount

    local_squares = sum(
        (portion(member, jnp.sum(grads[member] * grads[member])) for member in range(8))
    )
    local_weight_sq = [
        portion(member, jnp.sum(weights[member] * weights[member])) for member in range(6)
    ]
    sums = links.total(jnp.stack([local_squares] + local_weight_sq))
    squares, weight_sq = sums[0], sums[1:]
    global_norm = jnp.sqrt(squares)
    clip = 0.3 * math.sqrt(PARAMS) / (global_norm + 1e-06)
    pending = []
    local_update_sq = []
    for member in range(8):
        scaled = grads[member] * clip
        first_new = BETA * firsts[member] + (1.0 - BETA) * scaled
        second_new = BETA * seconds[member] + (1.0 - BETA) * scaled * scaled
        step_value = first_new / (jnp.sqrt(second_new) + EPS_ADAM)
        if member < 6:
            step_value = step_value + DECAY_WEIGHT * weights[member]
            local_update_sq.append(portion(member, jnp.sum(step_value * step_value)))
        pending.append((first_new, second_new, step_value))
    update_sq = links.total(jnp.stack(local_update_sq))
    weight_norm = jnp.sqrt(weight_sq)
    update_norm = jnp.sqrt(update_sq)
    trust = weight_norm / (update_norm + 1e-06)
    lamb_stats = jnp.stack([weight_norm, update_norm, trust], axis=1)
    results = []
    for member in range(8):
        first_new, second_new, step_value = pending[member]
        if member < 6:
            updated = weights[member] - RATE_MATRIX * trust[member] * step_value
        else:
            updated = weights[member] - RATE_VECTOR * step_value
        results += [updated, updated.astype(BF), first_new, second_new]
    return (out_state, grad_history, global_norm, lamb_stats, *results)


def solution(mesh):
    rows, columns, whole = P("dp", None), P(None, "dp"), P()
    middle = P(None, "dp", None)
    matrices = (rows,) * 5 + (whole,) + (columns,) * 2
    moments = tuple(spec for spec in matrices for _ in range(2))
    results = tuple(spec for spec in matrices for _ in range(4))
    return jax.shard_map(
        functools.partial(program, mesh.shape["dp"]),
        mesh=mesh,
        in_specs=(middle, rows, P("dp"), whole) + matrices + moments,
        out_specs=(rows, middle, whole, whole) + results,
        check_vma=False,
    )
```

```python
import functools
import math

import jax
import jax.numpy as jnp
from jax import lax
from jax.experimental import pallas as pl
from jax.experimental.pallas import tpu as pltpu
from jax.sharding import PartitionSpec as P

HD = 128
ROT = 32
PARAMS = 50416912

EPS_NORM = 1e-05
EPS_ADAM = 1e-06
DECAY_WEIGHT = 0.01
RATE_MATRIX = 0.3
RATE_VECTOR = 0.25
BETA = 0.5
NEGATIVE = -1e30
COST_SCALE = 200e3

BF = jnp.bfloat16
F32 = jnp.float32
TURNS = (0, 2, 1, 3)


def dot(left, right):
    return jnp.dot(left, right, preferred_element_type=F32)


def dot_tn(left, right):
    return lax.dot_general(left, right, (((0,), (0,)), ((), ())), preferred_element_type=F32)


def dot_nt(left, right):
    return lax.dot_general(left, right, (((1,), (1,)), ((), ())), preferred_element_type=F32)


def standardise(values):
    centred = values - jnp.mean(values, axis=-1, keepdims=True)
    scale = lax.rsqrt(jnp.mean(centred * centred, axis=-1, keepdims=True) + EPS_NORM)
    return centred * scale, scale


def norm_back(grad_xhat, xhat, scale):
    return scale * (
        grad_xhat
        - jnp.mean(grad_xhat, axis=-1, keepdims=True)
        - xhat * jnp.mean(grad_xhat * xhat, axis=-1, keepdims=True)
    )


def gelu_both(values):
    phi = 0.5 * (1.0 + lax.erf(values * math.sqrt(0.5)))
    bell = jnp.exp(-0.5 * values * values) * (1.0 / math.sqrt(2.0 * math.pi))
    return values * phi, phi + values * bell


def after(value, *first):
    return lax.optimization_barrier((value, first))[0]


SMEM = pl.BlockSpec(memory_space=pltpu.SMEM)


def fixed(array):
    shape = array.shape
    return pl.BlockSpec(
        shape, lambda *_: (0,) * len(shape), pipeline_mode=pl.Buffered(1)
    )


def run(kernel, cost, grid, ins, outs, scratch=()):
    return pl.pallas_call(
        kernel,
        grid=grid,
        in_specs=[spec for _, spec in ins],
        out_specs=[spec for _, _, spec in outs],
        out_shape=[jax.ShapeDtypeStruct(shape, kind) for shape, kind, _ in outs],
        scratch_shapes=list(scratch),
        compiler_params=pltpu.CompilerParams(vmem_limit_bytes=56 * 1024 * 1024),
        cost_estimate=pl.CostEstimate(
            flops=1024, bytes_accessed=int(COST_SCALE * cost), transcendentals=0
        ),
    )(*(array for array, _ in ins))


class Order:
    def __init__(self, where_ref, outer, block, quarter):
        self.rank, self.y = where_ref[0], where_ref[1]
        self.outer, self.block, self.quarter = outer, block, quarter

    def relative(self, k):
        start = (((k % 2) ^ self.y) * self.outer + k // 2) * self.block
        return pl.ds(pl.multiple_of(start, self.block), self.block)

    def natural(self, k):
        return slice(k * self.block, (k + 1) * self.block)

    def blocks(self):
        return range(2 * self.outer)

    def quarter_of(self, d):
        start = (self.rank ^ TURNS[d]) * self.quarter
        return pl.ds(pl.multiple_of(start, self.quarter), self.quarter)


def mixing_forward_kernel(
    order, where, h, w_mix, gain, bias, mixer, streams, normed, coef_out, pre_out
):
    order = order(where)
    hist_len, rows, width = h.shape
    step = 512
    xhat, _ = standardise(h[hist_len - 1].astype(F32))
    mix_normed = (xhat * gain[0:1, :]).astype(BF)
    pre = dot_nt(mix_normed, w_mix[...])
    hidden = gelu_both(pre)[0].astype(BF)
    coef = dot(hidden, mixer[...])
    pre_out[...] = pre
    coef_out[...] = coef
    for start in range(0, width, step):
        lanes = slice(start, start + step)
        parts = [h[j, :, lanes].astype(F32) for j in range(hist_len)]
        for a in range(4):
            first = a * hist_len
            total = coef[:, first : first + 1] * parts[0]
            for j in range(1, hist_len):
                total = total + coef[:, first + j : first + j + 1] * parts[j]
            streams[a, :, lanes] = total
    for a in range(3):
        xhat, _ = standardise(streams[a])
        low = (xhat * gain[1:2, :] + bias[0:1, :]).astype(BF)
        for k in order.blocks():
            normed[a, :, order.relative(k)] = low[:, order.natural(k)]


def turn(values, cos_table, sin_table):
    half_width = ROT // 2
    lane = lax.broadcasted_iota(jnp.int32, values.shape, 1)
    partner = jnp.where(
        lane < half_width,
        pltpu.roll(values, HD - half_width, axis=1),
        pltpu.roll(values, half_width, axis=1),
    )
    return values * cos_table + partner * sin_table


def head_scores(query, key):
    seq_len = query.shape[0]
    scores = dot_nt(query, key) * (1.0 / math.sqrt(HD))
    row = lax.broadcasted_iota(jnp.int32, (seq_len, seq_len), 0)
    column = lax.broadcasted_iota(jnp.int32, (seq_len, seq_len), 1)
    scores = jnp.where(row >= column, scores, NEGATIVE)
    exponent = jnp.exp(scores - jnp.max(scores, axis=-1, keepdims=True))
    return exponent / jnp.sum(exponent, axis=-1, keepdims=True)


def attention_forward_kernel(*refs):
    normed, (own, other, cos, sin) = refs[:4], refs[4:8]
    attended, query_rot, key_rot, value, made, held, arrived = refs[8:]
    quarter = attended.shape[1]
    half = own.shape[0]
    seq_len = cos.shape[0]
    copies = [
        pltpu.make_async_copy(normed[d], held.at[d], arrived.at[d]) for d in range(4)
    ]
    for copy in copies:
        copy.start()
    cos_table, sin_table = cos[...], sin[...]
    for d in range(4):
        copies[d].wait()
        rows = slice(d * seq_len, (d + 1) * seq_len)
        for a in range(3):
            lanes = slice(a * quarter, (a + 1) * quarter)
            made[a] = dot(held[d, a, :, :half], own[:, lanes]) + dot(
                held[d, a, :, half:], other[:, lanes]
            )
        value[rows, :] = made[2].astype(BF)
        for head in range(quarter // HD):
            lanes = slice(head * HD, (head + 1) * HD)
            query = turn(made[0, :, lanes], cos_table, sin_table).astype(BF)
            key = turn(made[1, :, lanes], cos_table, sin_table).astype(BF)
            query_rot[rows, lanes] = query
            key_rot[rows, lanes] = key
            probs = head_scores(query, key).astype(BF)
            attended[rows, lanes] = dot(probs, value[rows, lanes]).astype(BF)


def attention_backward_kernel(q, k, v, g, own, other, cos, sin, grads, *backs):
    quarter = q.shape[1]
    half = own.shape[0]
    scale = 1.0 / math.sqrt(HD)
    cos_table, sin_table = cos[...], -sin[...]
    for head in range(quarter // HD):
        lanes = slice(head * HD, (head + 1) * HD)
        query, key, grad = q[:, lanes], k[:, lanes], g[:, lanes]
        probs = head_scores(query, key)
        grad_probs = dot_nt(grad, v[:, lanes])
        centre = jnp.sum(probs * grad_probs, axis=-1, keepdims=True)
        grad_scores = (probs * (grad_probs - centre)).astype(BF)
        grads[0, :, lanes] = turn(dot(grad_scores, key) * scale, cos_table, sin_table).astype(BF)
        grads[1, :, lanes] = turn(
            dot_tn(grad_scores, query) * scale, cos_table, sin_table
        ).astype(BF)
        grads[2, :, lanes] = dot_tn(probs.astype(BF), grad).astype(BF)

    def send(back):
        for a in range(3):
            columns = slice(a * quarter, (a + 1) * quarter)
            back[a, :, :half] = dot_nt(grads[a], own[:, columns]).astype(BF)
            back[a, :, half:] = dot_nt(grads[a], other[:, columns]).astype(BF)

    for step in range(2):
        pl.when(pl.program_id(0) == step)(functools.partial(send, backs[step]))


def residual_kernel(order, where, *refs):
    order = order(where)
    parts, weights = refs[:4], refs[4:12]
    stream, gain, bias, residual, normed, attended, natural = refs[12:]
    half = weights[0].shape[0]
    for d in range(4):
        natural[:, order.quarter_of(d)] = parts[d][...]
    for k in order.blocks():
        attended[:, order.relative(k)] = natural[:, order.natural(k)]
    for d in range(4):
        columns = order.quarter_of(d)
        residual[:, columns] = (
            stream[0, :, columns]
            + dot(attended[:, :half], weights[2 * d][...])
            + dot(attended[:, half:], weights[2 * d + 1][...])
        )
    xhat, _ = standardise(residual[...])
    low = (xhat * gain[2:3, :] + bias[1:2, :]).astype(BF)
    for k in order.blocks():
        normed[:, order.relative(k)] = low[:, order.natural(k)]


def up_kernel(*refs):
    rows, (own, other, activated, slope) = refs[:4], refs[4:]
    half = own.shape[0]
    seq_len = rows[0].shape[0]
    for d in range(4):
        up = dot(rows[d][:, :half], own[...]) + dot(rows[d][:, half:], other[...])
        active, back = gelu_both(up)
        activated[d * seq_len : (d + 1) * seq_len, :] = active.astype(BF)
        slope[d * seq_len : (d + 1) * seq_len, :] = back


def down_grad_kernel(activated, *refs):
    rows, out = refs[:4], refs[4]
    seq_len = rows[0].shape[0]
    total = dot_tn(activated[:seq_len, :], rows[0][...])
    for d in range(1, 4):
        total = total + dot_tn(activated[d * seq_len : (d + 1) * seq_len, :], rows[d][...])
    out[...] = total.astype(BF)


def hidden_back_kernel(*refs):
    rows, (weight, slope, out) = refs[:4], refs[4:]
    seq_len = rows[0].shape[0]
    for d in range(4):
        part = slice(d * seq_len, (d + 1) * seq_len)
        out[part, :] = (dot_nt(rows[d][...], weight[...]) * slope[part, :]).astype(BF)


def down_kernel(activated, weight, *outs):
    total = dot(activated[...], weight[...]).astype(BF)
    seq_len = outs[0].shape[0]
    for d in range(4):
        outs[d][...] = total[d * seq_len : (d + 1) * seq_len]


def up_grad_kernel(*refs):
    rows, (grad, out) = refs[:4], refs[4:]
    seq_len = rows[0].shape[0]
    total = dot_tn(rows[0][...], grad[:seq_len, :])
    for d in range(1, 4):
        total = total + dot_tn(rows[d][...], grad[d * seq_len : (d + 1) * seq_len, :])
    out[...] = total.astype(BF)


def normed_back_kernel(pair, grad, own, other, *outs):
    step, steps = pl.program_id(0), pl.num_programs(0)
    seq_len = outs[0].shape[0]

    def send(weight):
        for d, out in zip(pair, outs):
            rows = slice(d * seq_len, (d + 1) * seq_len)
            out[...] = dot_nt(grad[rows, :], weight[...]).astype(BF)

    pl.when(step < steps // 2)(functools.partial(send, own))
    pl.when(step >= steps // 2)(functools.partial(send, other))


def residual_back_kernel(order, where, *refs):
    order = order(where)
    residual, gain, mine, from_core, from_x, grad_out = refs[:6]
    weights = refs[6:14]
    grad, grad_gain, grad_bias = refs[14:17]
    parts, wide, low = refs[17:21], refs[21], refs[22]
    half = weights[0].shape[0]
    for k in order.blocks():
        source = order.relative(k)
        wide[:, order.natural(k)] = (
            mine[:, source].astype(F32)
            + from_core[:, source].astype(F32)
            + from_x[:, source].astype(F32)
        )
    xhat, scale = standardise(residual[...])
    grad_y = wide[...]
    grad_gain[...] = jnp.sum(grad_y * xhat, axis=0, keepdims=True)
    grad_bias[...] = jnp.sum(grad_y, axis=0, keepdims=True)
    grad_x = norm_back(grad_y * gain[2:3, :], xhat, scale)
    grad[...] = (grad_out[...].astype(F32) + grad_x).astype(BF)
    for s in range(2):
        total = dot_nt(grad[:, order.quarter_of(0)], weights[s][...])
        for d in range(1, 4):
            total = total + dot_nt(grad[:, order.quarter_of(d)], weights[2 * d + s][...])
        low[:, s * half : (s + 1) * half] = total.astype(BF)
    for k in order.blocks():
        wide[:, order.natural(k)] = low[:, order.relative(k)].astype(F32)
    for d in range(4):
        parts[d][...] = wide[:, order.quarter_of(d)].astype(BF)


def out_grad_kernel(order, where, attended, grad, *outs):
    order = order(where)
    for d in range(4):
        outs[d][...] = dot_tn(attended[...], grad[:, order.quarter_of(d)]).astype(BF)


def in_grad_kernel(*refs):
    normed, (even, odd, out) = refs[:4], refs[4:]
    seq_len = normed[0].shape[1]
    total = None
    for d in range(4):
        rows = slice(d // 2 * seq_len, (d // 2 + 1) * seq_len)
        part = dot_tn(normed[d][0], (odd if d % 2 else even)[0, rows, :])
        total = part if total is None else total + part
    out[...] = total.astype(BF)


def mixing_backward_kernel(order, where, *refs):
    order = order(where)
    h, streams, coef_in, pre_in, mine, from_core, from_x, grad_residual = refs[:8]
    w_mix, gain, mixer = refs[8:11]
    grad_history, grad_mix, grad_mixer, grad_gains, grad_bias = refs[11:16]
    grad_streams = refs[16]
    hist_len, rows, width = h.shape
    step = 512

    @pl.when(pl.program_id(0) == 0)
    def _():
        grad_mix[...] = jnp.zeros_like(grad_mix)
        grad_mixer[...] = jnp.zeros_like(grad_mixer)
        grad_gains[...] = jnp.zeros_like(grad_gains)
        grad_bias[...] = jnp.zeros_like(grad_bias)

    for a in range(3):
        for k in order.blocks():
            source = order.relative(k)
            grad_streams[a, :, order.natural(k)] = (
                mine[a, :, source].astype(F32)
                + from_core[a, :, source].astype(F32)
                + from_x[a, :, source].astype(F32)
            )
        xhat, scale = standardise(streams[a])
        grad_y = grad_streams[a]
        grad_gains[1:2, :] += jnp.sum(grad_y * xhat, axis=0, keepdims=True)
        grad_bias[...] += jnp.sum(grad_y, axis=0, keepdims=True)
        grad_streams[a] = norm_back(grad_y * gain[1:2, :], xhat, scale)
    grad_streams[3] = grad_residual[...].astype(F32)

    coef = coef_in[...]
    columns = coef.shape[1]
    sums = [jnp.zeros((rows, 128), F32) for _ in range(columns)]
    for start in range(0, width, step):
        lanes = slice(start, start + step)
        grads = [grad_streams[a, :, lanes] for a in range(4)]
        for j in range(hist_len):
            part = h[j, :, lanes].astype(F32)
            back = coef[:, j : j + 1] * grads[0]
            for a in range(1, 4):
                at = a * hist_len + j
                back = back + coef[:, at : at + 1] * grads[a]
            for a in range(4):
                product = grads[a] * part
                folded = product[:, 0:128]
                for lane in range(128, step, 128):
                    folded = folded + product[:, lane : lane + 128]
                sums[a * hist_len + j] = sums[a * hist_len + j] + folded
            if j < hist_len - 1:
                grad_history[j, :, lanes] = back.astype(BF)
            else:
                grad_streams[3, :, lanes] = back
    lane = lax.broadcasted_iota(jnp.int32, (rows, columns), 1)
    grad_coef = jnp.zeros((rows, columns), F32)
    for at in range(columns):
        grad_coef = jnp.where(lane == at, jnp.sum(sums[at], axis=-1, keepdims=True), grad_coef)
    grad_coef = grad_coef.astype(BF)
    hidden, slope = gelu_both(pre_in[...])
    hidden = hidden.astype(BF)
    grad_mixer[...] += dot_tn(hidden, grad_coef)
    grad_pre = (dot_nt(grad_coef, mixer[...]) * slope).astype(BF)
    xhat, scale = standardise(h[hist_len - 1].astype(F32))
    grad_mix[...] += dot_tn(grad_pre, (xhat * gain[0:1, :]).astype(BF))
    grad_y = dot(grad_pre, w_mix[...])
    grad_gains[0:1, :] += jnp.sum(grad_y * xhat, axis=0, keepdims=True)
    grad_current = norm_back(grad_y * gain[0:1, :], xhat, scale)
    grad_history[hist_len - 1] = (grad_streams[3] + grad_current).astype(BF)


def rotary_tables(seq_len):
    half_width = ROT // 2
    frequency = 10000.0 ** (-(2.0 * jnp.arange(half_width, dtype=F32)) / ROT)
    angles = jnp.arange(seq_len, dtype=F32)[:, None] * frequency[None, :]
    cosine, sine = jnp.cos(angles), jnp.sin(angles)
    rest = HD - ROT
    cos_table = jnp.concatenate([cosine, cosine, jnp.ones((seq_len, rest), F32)], axis=1)
    sin_table = jnp.concatenate([-sine, sine, jnp.zeros((seq_len, rest), F32)], axis=1)
    return cos_table, sin_table


def moments_kernel(clip_ref, *refs):
    clip = clip_ref[0]
    step = 512

    @pl.when(pl.program_id(0) == 0)
    def _():
        for member in range(4):
            refs[24][member] = 0.0

    for member in range(4):
        grad, first, second, weight = refs[4 * member : 4 * member + 4]
        first_out, second_out = refs[16 + 2 * member : 18 + 2 * member]
        total = 0.0
        for start in range(0, grad.shape[1], step):
            lanes = slice(start, start + step)
            scaled = grad[:, lanes].astype(F32) * clip
            first_new = BETA * first[:, lanes] + (1.0 - BETA) * scaled
            second_new = BETA * second[:, lanes] + (1.0 - BETA) * scaled * scaled
            first_out[:, lanes] = first_new
            second_out[:, lanes] = second_new
            change = first_new / (jnp.sqrt(second_new) + EPS_ADAM) + DECAY_WEIGHT * weight[:, lanes]
            total = total + jnp.sum(change * change, axis=0, keepdims=True)
        refs[24][member] = refs[24][member] + jnp.sum(total)


def apply_kernel(trust_ref, *refs):
    step = 512
    for member in range(4):
        first, second, weight = refs[3 * member : 3 * member + 3]
        out, low = refs[12 + 2 * member : 14 + 2 * member]
        rate = RATE_MATRIX * trust_ref[member]
        for start in range(0, weight.shape[1], step):
            lanes = slice(start, start + step)
            old = weight[:, lanes]
            change = first[:, lanes] / (jnp.sqrt(second[:, lanes]) + EPS_ADAM) + DECAY_WEIGHT * old
            new = old - rate * change
            out[:, lanes] = new
            low[:, lanes] = new.astype(BF)


class Links:
    def __init__(self, devices, width):
        self.devices = devices
        index = lax.axis_index("dp")
        self.core = index & 1
        self.x = (index >> 1) & 1
        self.rank = index & 3
        self.index = index
        self.y_bit = 2
        self.block = 4 * width // devices
        while self.block % 128:
            self.y_bit += 1
            self.block *= 2
        self.inner = 1 << (self.y_bit - 2)
        self.outer = width // (2 * self.block)
        self.y = (index >> self.y_bit) & 1
        self.where = jnp.stack([self.rank, self.y]).astype(jnp.int32)
        groups = {}
        for j in range(devices):
            groups.setdefault((j & 3, (j >> self.y_bit) & 1), []).append(j)
        self.z_groups = list(groups.values())

    def swap(self, value, bit):
        return lax.ppermute(value, "dp", [(j, j ^ bit) for j in range(self.devices)])

    def swap_core(self, value):
        return self.swap(value, 1)

    def swap_x(self, value):
        return self.swap(value, 2)

    def swap_y(self, value):
        return self.swap(value, 1 << self.y_bit)

    def gather(self, value, groups):
        return lax.all_gather(value, "dp", axis=0, tiled=True, axis_index_groups=groups)

    def reduce(self, value, groups):
        return lax.psum_scatter(
            value, "dp", scatter_dimension=0, tiled=True, axis_index_groups=groups
        )

    def total(self, value):
        bit = 1
        while bit < self.devices:
            pair = value + self.swap(value, bit)
            if 2 * bit < self.devices:
                pair = pair + (self.swap(value, 2 * bit) + self.swap(value, 3 * bit))
            value = pair
            bit *= 4
        return value

    def to_absolute(self, parts):
        own, across_x, across_core, across_both = parts
        low_x = self.x == 0
        core_own = (jnp.where(low_x, own, across_x), jnp.where(low_x, across_x, own))
        core_other = (
            jnp.where(low_x, across_core, across_both),
            jnp.where(low_x, across_both, across_core),
        )
        low_core = self.core == 0
        ordered = []
        for mine, other in zip(core_own, core_other):
            ordered.append(jnp.where(low_core, mine, other))
            ordered.append(jnp.where(low_core, other, mine))
        return ordered

    def to_relative(self, parts):
        low_x, low_core = self.x == 0, self.core == 0
        near = [jnp.where(low_x, parts[c], parts[2 + c]) for c in (0, 1)]
        far = [jnp.where(low_x, parts[2 + c], parts[c]) for c in (0, 1)]
        return [
            jnp.where(low_core, near[0], near[1]),
            jnp.where(low_core, far[0], far[1]),
            jnp.where(low_core, near[1], near[0]),
            jnp.where(low_core, far[1], far[0]),
        ]

    def group_gather(self, value):
        across_x = self.swap_x(value)
        return [value, across_x, self.swap_core(value), self.swap_core(across_x)]

    def group_exchange(self, parts):
        own, for_x, for_core, for_both = parts
        from_both = self.swap_x(for_both)
        from_x = self.swap_x(for_x)
        return [own, from_x, self.swap_core(for_core), self.swap_core(from_both)]

    def group_reduce(self, own, for_x, for_core, for_both, *ties):
        from_both = self.swap_core(for_both)
        for_x = (for_x.astype(F32) + from_both.astype(F32)).astype(BF)
        return self.swap_core(for_core), self.swap_x(after(for_x, *ties)), for_x


def program(
    devices,
    history,
    d_out,
    group_ids,
    group_weight,
    attn_in,
    attn_out,
    ffn_up,
    ffn_down,
    mixer_in,
    mixer_out,
    norm_gain,
    norm_bias,
    first_attn_in,
    second_attn_in,
    first_attn_out,
    second_attn_out,
    first_ffn_up,
    second_ffn_up,
    first_ffn_down,
    second_ffn_down,
    first_mixer_in,
    second_mixer_in,
    first_mixer_out,
    second_mixer_out,
    first_norm_gain,
    second_norm_gain,
    first_norm_bias,
    second_norm_bias,
):
    hist_len, seq_len, width = history.shape
    links = Links(devices, width)
    order = functools.partial(
        Order, outer=links.outer, block=links.block, quarter=width // 4
    )
    with_order = lambda kernel: functools.partial(kernel, order)
    where = (links.where, SMEM)
    quarter, half = width // 4, width // 2
    rows = width // devices
    hidden = ffn_down.shape[0] * devices
    units = hidden // devices
    share = hidden // 4
    four = 4 * seq_len
    whole = lambda array: (array, fixed(array))

    low_attn = attn_in.astype(BF).reshape(rows, 3, 4, quarter)
    low_out = attn_out.astype(BF).reshape(rows, 1, 4, quarter)
    by_rank = jnp.concatenate([low_attn, low_out], axis=1)
    by_rank = [by_rank[:, :, r].reshape(rows, width) for r in range(4)]
    attn_parts = links.group_exchange(links.to_relative(by_rank))
    attn_block = jnp.concatenate(links.to_absolute(attn_parts), axis=0)

    low_up = ffn_up.astype(BF).reshape(rows, links.outer, 2, links.inner, 4, units)
    low_up = jnp.transpose(low_up, (4, 0, 1, 3, 2, 5)).reshape(4, rows, share)
    own, for_x, for_core, for_both = after(links.to_relative(list(low_up)), attn_parts[1])
    from_both = after(links.swap_x(for_both), attn_block)
    up_parts = [own, links.swap_x(for_x), links.swap_core(for_core), links.swap_core(from_both)]
    up_block = jnp.concatenate(links.to_absolute(up_parts), axis=0)

    low_down = ffn_down.astype(BF)
    other_down = links.swap_y(low_down)
    low_y = links.y == 0

    attn_own = links.gather(attn_block, links.z_groups)
    attn_other = links.swap_y(attn_own)
    up_own = links.gather(up_block, links.z_groups)
    up_other = links.swap_y(up_own)

    hidden_mix = mixer_in.shape[1]
    pack = jnp.concatenate([mixer_in.T, norm_gain, norm_bias], axis=0).astype(BF)
    bit = 1
    while bit < devices:
        other = links.swap(pack, bit)
        low = (links.index & bit) == 0
        pack = jnp.concatenate([jnp.where(low, pack, other), jnp.where(low, other, pack)], axis=1)
        bit *= 2
    w_mixer_in = pack[:hidden_mix]
    gain_table = pack[hidden_mix : hidden_mix + 3].astype(F32)
    bias_table = pack[hidden_mix + 3 :].astype(F32)
    mixer_low = mixer_out.astype(BF)

    tile = 64
    steps = (seq_len // tile,)
    columns = mixer_out.shape[1]
    row_tile = lambda *lead: pl.BlockSpec(
        lead + (tile, width), lambda t: (0,) * len(lead) + (t, 0)
    )
    narrow = pl.BlockSpec((tile, columns), lambda t: (t, 0))
    pre_narrow = pl.BlockSpec((tile, hidden_mix), lambda t: (t, 0))
    streams, normed, coef, mix_pre = run(
        with_order(mixing_forward_kernel),
        14,
        steps,
        [
            where,
            (history, row_tile(hist_len)),
            whole(w_mixer_in),
            whole(gain_table),
            whole(bias_table),
            whole(mixer_low),
        ],
        [
            ((4, seq_len, width), F32, row_tile(4)),
            ((3, seq_len, width), BF, row_tile(3)),
            ((seq_len, columns), F32, narrow),
            ((seq_len, hidden_mix), F32, pre_narrow),
        ],
    )

    low_down, other_down = after((low_down, other_down), normed)
    down_block = jnp.concatenate(
        [jnp.where(low_y, low_down, other_down), jnp.where(low_y, other_down, low_down)], axis=0
    )
    w_down = links.gather(down_block, links.z_groups)

    tables = [whole(table) for table in rotary_tables(seq_len)]
    normed_four = links.group_gather(normed)
    attn_weights = [
        (
            array,
            pl.BlockSpec((half, 3 * quarter), lambda s: (0, 0), pipeline_mode=pl.Buffered(1)),
        )
        for array in (attn_own, attn_other)
    ]
    out_mine = [array[:, 3 * quarter :] for array in (attn_own, attn_other)]
    out_x = [links.swap_x(array) for array in out_mine]
    group_count = group_weight.shape[0]
    seq_weight = jnp.sum(
        jnp.where(jnp.arange(group_count, dtype=jnp.int32) == group_ids[0], group_weight, 0.0)
    )
    grad_out = (d_out.astype(F32) * seq_weight).astype(BF)
    grad_out = after(grad_out, normed_four[1])
    grad_out_x = links.swap_x(grad_out)
    seq_block = pl.BlockSpec((seq_len, quarter), lambda s: (s, 0))
    attn_other_now = after(attn_other, grad_out_x)
    anywhere = pl.BlockSpec(memory_space=pl.ANY)
    four_quarter = pl.BlockSpec((four, quarter), lambda _: (0, 0))
    attended, query_rot, key_rot, value = run(
        attention_forward_kernel,
        16,
        (1,),
        [(part, anywhere) for part in normed_four]
        + [(attn_own, attn_weights[0][1]), (attn_other_now, attn_weights[0][1])]
        + tables,
        [((four, quarter), BF, four_quarter)] * 4,
        [
            pltpu.VMEM((3, seq_len, quarter), F32),
            pltpu.VMEM((4, 3, seq_len, width), BF),
            pltpu.SemaphoreType.DMA((4,)),
        ],
    )
    out_x = after(out_x, attended)
    out_halves = [
        [out_mine[k], out_x[k], links.swap_core(out_mine[k]), links.swap_core(out_x[k])]
        for k in range(2)
    ]
    w_out = [out_halves[k][d] for d in range(4) for k in range(2)]
    attended = links.group_exchange(
        [attended[d * seq_len : (d + 1) * seq_len] for d in range(4)]
    )
    one_row = ((1, width), F32, pl.BlockSpec((1, width), lambda *_: (0, 0)))
    full = lambda kind: (
        (seq_len, width),
        kind,
        pl.BlockSpec((seq_len, width), lambda *_: (0, 0)),
    )
    residual, ffn_normed, attended_rel = run(
        with_order(residual_kernel),
        9,
        (1,),
        [where]
        + [whole(part) for part in attended]
        + [whole(part) for part in w_out]
        + [
            (
                streams,
                pl.BlockSpec(
                    (1, seq_len, width), lambda _: (3, 0, 0), pipeline_mode=pl.Buffered(1)
                ),
            ),
            whole(gain_table),
            whole(bias_table),
        ],
        [full(F32), full(BF), full(BF)],
        [pltpu.VMEM((seq_len, width), BF)],
    )

    ffn_four = links.group_gather(ffn_normed)
    wide = 256
    column_tile = lambda count: pl.BlockSpec((count, wide), lambda t: (0, t))
    line_tile = lambda count: pl.BlockSpec((wide, count), lambda t: (t, 0))
    activated, slope = run(
        up_kernel,
        17,
        (share // wide,),
        [whole(part) for part in ffn_four]
        + [(up_own, column_tile(half)), (up_other, column_tile(half))],
        [((four, share), BF, column_tile(four)), ((four, share), F32, column_tile(four))],
    )

    grad_out_x = after(grad_out_x, activated)
    grad_out_four = [
        grad_out,
        grad_out_x,
        links.swap_core(grad_out),
        links.swap_core(grad_out_x),
    ]

    (grad_down,) = run(
        down_grad_kernel,
        14,
        (share // wide,),
        [(activated, column_tile(four))] + [whole(part) for part in grad_out_four],
        [((share, width), BF, line_tile(width))],
    )
    down_sums = links.reduce(grad_down, links.z_groups)

    (grad_up,) = run(
        hidden_back_kernel,
        16,
        (share // wide,),
        [whole(part) for part in grad_out_four]
        + [(w_down, line_tile(width)), (after(slope, grad_down), column_tile(four))],
        [((four, share), BF, column_tile(four))],
    )

    def whole_rows(block):
        parts = list(block.reshape(4, rows, block.shape[1]))
        parts = links.to_absolute(links.group_exchange(links.to_relative(parts)))
        return jnp.stack(parts, axis=1)

    tiles = half // wide

    def normed_back(pair, grad):
        return run(
            functools.partial(normed_back_kernel, pair),
            11,
            (2 * tiles,),
            [
                whole(grad),
                (up_own, pl.BlockSpec((wide, share), lambda t: (jnp.minimum(t, tiles - 1), 0))),
                (up_other, pl.BlockSpec((wide, share), lambda t: (jnp.maximum(t - tiles, 0), 0))),
            ],
            [((seq_len, width), BF, column_tile(seq_len))] * 2,
        )

    def up_grad(first, count, grad):
        block = pl.BlockSpec((seq_len, wide), lambda t: (0, first + t))
        (out,) = run(
            up_grad_kernel,
            9,
            (count,),
            [(part, block) for part in ffn_four] + [whole(grad)],
            [((count * wide, share), BF, line_tile(share))],
        )
        return out

    for_x, for_both = normed_back((1, 3), grad_up)
    up_first = up_grad(tiles, 1, after(grad_up, for_both))
    up_theirs_first = links.swap_y(up_first)
    up_rest = up_grad(tiles + 1, tiles - 1, after(grad_up, up_first))
    up_theirs_rest = links.swap_y(up_rest)
    own, for_core = normed_back((0, 2), after(grad_up, up_rest))
    up_grad_own = up_grad(0, tiles, after(grad_up, own))
    from_core, from_x, _ = links.group_reduce(own, for_x, for_core, for_both)
    from_x = after(from_x, up_grad_own, up_theirs_first)
    part_out = ((seq_len, quarter), BF, pl.BlockSpec((seq_len, quarter), lambda _: (0, 0)))
    back = run(
        with_order(residual_back_kernel),
        11,
        (1,),
        [
            where,
            whole(residual),
            whole(gain_table),
            whole(own),
            whole(from_core),
            whole(from_x),
            whole(grad_out),
        ]
        + [whole(part) for part in w_out],
        [full(BF), one_row, one_row] + [part_out] * 4,
        [pltpu.VMEM((seq_len, width), F32), pltpu.VMEM((seq_len, width), BF)],
    )
    grad_residual, grad_gain_ffn, grad_bias_ffn = back[:3]

    heads_own, for_x, for_core, for_both = back[3:]
    from_both, from_x = links.swap_x(for_both), links.swap_x(for_x)
    grad_heads = [
        heads_own,
        from_x,
        links.swap_core(for_core),
        links.swap_core(from_both),
    ]

    line = 512
    out_parts = run(
        with_order(out_grad_kernel),
        7,
        (width // line,),
        [
            where,
            (attended_rel, pl.BlockSpec((seq_len, line), lambda t: (0, t))),
            whole(grad_residual),
        ],
        [((width, quarter), BF, pl.BlockSpec((line, quarter), lambda t: (t, 0)))] * 4,
    )
    out_parts = after(out_parts, from_x, from_both)
    out_both, out_core = links.swap_core(out_parts[3]), links.swap_core(out_parts[2])

    def attention_back(first, *ties):
        heads = jnp.concatenate([grad_heads[first], grad_heads[first + 2]], axis=0)
        block = pl.BlockSpec((seq_len, quarter), lambda s: (first + 2 * s, 0))
        back_out = (
            (3, seq_len, width),
            BF,
            pl.BlockSpec((3, seq_len, width), lambda s: (0, 0, 0)),
        )
        return run(
            attention_backward_kernel,
            15,
            (2,),
            [(query_rot, block), (key_rot, block), (value, block)]
            + [(after(heads, *ties), seq_block)]
            + attn_weights
            + tables,
            [
                (
                    (3, 2 * seq_len, quarter),
                    BF,
                    pl.BlockSpec((3, seq_len, quarter), lambda s: (0, s, 0)),
                ),
                back_out,
                back_out,
            ],
        )

    plus = lambda mine, theirs: (mine.astype(F32) + theirs.astype(F32)).astype(BF)
    proj_odd, for_x, for_both = attention_back(1)
    out_for_x = plus(out_parts[1], after(out_both, for_both))
    out_x = links.swap_x(out_for_x)
    proj_even, own, for_core = attention_back(0, out_for_x)
    from_core, from_x, for_x = links.group_reduce(own, for_x, for_core, for_both)
    proj_even = after(proj_even, for_x)

    def in_grad(s, proj):
        block = pl.BlockSpec((1, seq_len, wide), lambda a, t: (a, 0, s * tiles + t))
        proj_block = pl.BlockSpec((1, 2 * seq_len, quarter), lambda a, t: (a, 0, 0))
        (out,) = run(
            in_grad_kernel,
            12,
            (3, tiles),
            [(part, block) for part in normed_four] + [(proj, proj_block), (proj_odd, proj_block)],
            [((half, 3 * quarter), BF, pl.BlockSpec((wide, quarter), lambda a, t: (t, a)))],
        )
        return out

    in_grad_other = in_grad(1, proj_even)
    in_theirs = links.swap_y(in_grad_other)
    in_grad_own = in_grad(0, after(proj_even, in_grad_other))

    up_theirs = jnp.concatenate(
        [up_theirs_first, after(up_theirs_rest, in_grad_own, out_x)]
    )
    up_both = after(plus(up_grad_own, up_theirs), down_sums)
    up_sums = links.reduce(up_both, links.z_groups)
    out_x = after(out_x, up_both)
    out_grad = out_parts[0].astype(F32) + out_core.astype(F32) + out_x.astype(F32)
    out_theirs = links.swap_y(out_grad[half:].astype(BF))
    down_parts = run(
        down_kernel,
        14,
        (width // wide,),
        [whole(after(activated, up_both)), (w_down, column_tile(share))],
        [((seq_len, width), BF, column_tile(seq_len))] * 4,
    )
    down_core, down_x, down_for_x = links.group_reduce(*down_parts, from_x)
    out_state = (
        residual + down_parts[0].astype(F32) + down_core.astype(F32) + down_x.astype(F32)
    ).astype(BF)

    in_theirs = after(in_theirs, down_for_x)
    attn_both = jnp.concatenate(
        [plus(in_grad_own, in_theirs), plus(out_grad[:half], out_theirs)], axis=1
    )
    attn_both = after(attn_both, up_sums, from_x, from_core)
    attn_sums = links.reduce(attn_both, links.z_groups)

    fixed_out = lambda shape: (
        shape,
        F32,
        pl.BlockSpec(shape, lambda t: (0, 0)),
    )
    grad_history, grad_mixer_in, grad_mixer_out, grad_gains, grad_bias_attn = run(
        with_order(mixing_backward_kernel),
        25,
        steps,
        [
            where,
            (history, row_tile(hist_len)),
            (streams, row_tile(3)),
            (coef, narrow),
            (mix_pre, pre_narrow),
            (own, row_tile(3)),
            (from_core, row_tile(3)),
            (from_x, row_tile(3)),
            (after(grad_residual, attn_both), row_tile()),
            whole(w_mixer_in),
            whole(gain_table),
            whole(mixer_low),
        ],
        [
            ((hist_len, seq_len, width), BF, row_tile(hist_len)),
            fixed_out((hidden_mix, width)),
            fixed_out((hidden_mix, columns)),
            fixed_out((2, width)),
            fixed_out((1, width)),
        ],
        [pltpu.VMEM((4, tile, width), F32)],
    )

    down_sums, up_sums = after(down_sums, attn_both), after(up_sums, attn_both)
    down_sums = down_sums.reshape(2, units, width)
    down_mine = jnp.where(low_y, down_sums[0], down_sums[1])
    down_theirs = jnp.where(low_y, down_sums[1], down_sums[0])
    shard_down = down_mine.astype(F32) + links.swap_y(down_theirs).astype(F32)
    shard_up = jnp.transpose(
        whole_rows(up_sums).reshape(rows, 4, links.outer, links.inner, 2, units),
        (0, 2, 4, 3, 1, 5),
    ).reshape(rows, hidden)

    small = jnp.concatenate(
        [grad_mixer_in, grad_gains, grad_gain_ffn, grad_bias_attn, grad_bias_ffn], axis=0
    )
    small = after(small, shard_up, shard_down, down_x)
    bits = [links.y_bit] + [k for k in reversed(range(2, devices.bit_length() - 1)) if k != links.y_bit]
    pieces = small.reshape((small.shape[0],) + (2,) * (devices.bit_length() - 3) + (4 * rows,))
    left = list(reversed(range(2, devices.bit_length() - 1)))
    for k in bits:
        axis = 1 + left.index(k)
        left.remove(k)
        low = (links.index & (1 << k)) == 0
        first = lax.index_in_dim(pieces, 0, axis, keepdims=False)
        second = lax.index_in_dim(pieces, 1, axis, keepdims=False)
        pieces = jnp.where(low, first, second) + links.swap(
            jnp.where(low, second, first), 1 << k
        )
    small = pieces
    small = small + links.swap_x(small)
    small = small + links.swap_core(small)
    small = lax.dynamic_slice_in_dim(small, links.rank * rows, rows, axis=1)
    mixer_grad = links.total(grad_mixer_out)
    square = lambda array: jnp.sum(jnp.square(array.astype(F32)))
    early_squares = square(up_sums) + square(shard_down) + square(small)
    early_squares = early_squares + square(mixer_grad) / devices
    attn_sums = after(attn_sums, shard_up, early_squares)
    attn_rows = whole_rows(attn_sums).reshape(rows, 4, 4, quarter)
    attn_rows = jnp.transpose(attn_rows, (0, 2, 1, 3)).reshape(rows, 4 * width)
    shard_in, shard_out = attn_rows[:, : 3 * width], attn_rows[:, 3 * width :]
    grads = (
        shard_in,
        shard_out,
        shard_up,
        shard_down,
        small[:hidden_mix].T,
        mixer_grad,
        small[hidden_mix : hidden_mix + 3],
        small[hidden_mix + 3 :],
    )

    weights = (attn_in, attn_out, ffn_up, ffn_down, mixer_in, mixer_out, norm_gain, norm_bias)
    firsts = (
        first_attn_in,
        first_attn_out,
        first_ffn_up,
        first_ffn_down,
        first_mixer_in,
        first_mixer_out,
        first_norm_gain,
        first_norm_bias,
    )
    seconds = (
        second_attn_in,
        second_attn_out,
        second_ffn_up,
        second_ffn_down,
        second_mixer_in,
        second_mixer_out,
        second_norm_gain,
        second_norm_bias,
    )

    def portion(member, amount):
        return amount / devices if member == 5 else amount

    weights_later = after(weights, coef)
    local_squares = early_squares + square(attn_sums)
    local_weight_sq = [portion(member, square(weights_later[member])) for member in range(6)]
    sums = links.total(jnp.stack([local_squares] + local_weight_sq))
    squares, weight_sq = sums[0], sums[1:]
    global_norm = jnp.sqrt(squares)
    clip = 0.3 * math.sqrt(PARAMS) / (global_norm + 1e-06)
    parts = rows // 16
    slab = lambda array: pl.BlockSpec(
        (array.shape[0] // parts, array.shape[1]), lambda t: (t, 0)
    )
    slabs = lambda *arrays: [(array, slab(array)) for array in arrays]
    made = lambda array, kind: (array.shape, kind, slab(array))
    ins, outs = [(clip[None], SMEM)], []
    for member in range(4):
        ins += slabs(grads[member], firsts[member], seconds[member], weights[member])
        outs += [made(weights[member], F32)] * 2
    outs.append(((4,), F32, SMEM))
    moments = run(moments_kernel, 14, (parts,), ins, outs)
    firsts_new, seconds_new = list(moments[0:8:2]), list(moments[1:8:2])
    local_update_sq = moments[8]
    steps_small = []
    for member in range(4, 8):
        scaled = grads[member] * clip
        first_new = BETA * firsts[member] + (1.0 - BETA) * scaled
        second_new = BETA * seconds[member] + (1.0 - BETA) * scaled * scaled
        step_value = first_new / (jnp.sqrt(second_new) + EPS_ADAM)
        if member < 6:
            step_value = step_value + DECAY_WEIGHT * weights[member]
        firsts_new.append(first_new)
        seconds_new.append(second_new)
        steps_small.append(step_value)
    small_sq = [portion(4 + k, jnp.sum(steps_small[k] * steps_small[k])) for k in range(2)]
    update_sq = links.total(jnp.concatenate([local_update_sq, jnp.stack(small_sq)]))
    weight_norm = jnp.sqrt(weight_sq)
    update_norm = jnp.sqrt(update_sq)
    trust = weight_norm / (update_norm + 1e-06)
    lamb_stats = jnp.stack([weight_norm, update_norm, trust], axis=1)
    ins, outs = [(trust, SMEM)], []
    for member in range(4):
        ins += slabs(firsts_new[member], seconds_new[member], weights[member])
        outs += [made(weights[member], F32), made(weights[member], BF)]
    applied = run(apply_kernel, 10, (parts,), ins, outs)
    results = []
    for member in range(8):
        if member < 4:
            updated, low = applied[2 * member], applied[2 * member + 1]
        else:
            rate = RATE_MATRIX * trust[member] if member < 6 else RATE_VECTOR
            updated = weights[member] - rate * steps_small[member - 4]
            low = updated.astype(BF)
        results += [updated, low, firsts_new[member], seconds_new[member]]
    return (out_state, grad_history, global_norm, lamb_stats, *results)


def solution(mesh):
    rows, columns, whole = P("dp", None), P(None, "dp"), P()
    middle = P(None, "dp", None)
    matrices = (rows,) * 5 + (whole,) + (columns,) * 2
    moments = tuple(spec for spec in matrices for _ in range(2))
    results = tuple(spec for spec in matrices for _ in range(4))
    return jax.shard_map(
        functools.partial(program, mesh.shape["dp"]),
        mesh=mesh,
        in_specs=(middle, rows, P("dp"), whole) + matrices + moments,
        out_specs=(rows, middle, whole, whole) + results,
        check_vma=False,
    )
```

```python
import functools
import math

import jax
import jax.numpy as jnp
from jax import lax
from jax.experimental import pallas as pl
from jax.experimental.pallas import tpu as pltpu
from jax.sharding import PartitionSpec as P

HD = 128
ROT = 32
PARAMS = 50416912

EPS_NORM = 1e-05
EPS_ADAM = 1e-06
DECAY_WEIGHT = 0.01
RATE_MATRIX = 0.3
RATE_VECTOR = 0.25
BETA = 0.5
NEGATIVE = -1e30
COST_SCALE = 200e3
PLACE_COST = 450

BF = jnp.bfloat16
F32 = jnp.float32
TURNS = (0, 2, 1, 3)


def dot(left, right):
    return jnp.dot(left, right, preferred_element_type=F32)


def dot_tn(left, right):
    return lax.dot_general(left, right, (((0,), (0,)), ((), ())), preferred_element_type=F32)


def dot_nt(left, right):
    return lax.dot_general(left, right, (((1,), (1,)), ((), ())), preferred_element_type=F32)


def standardise(values):
    centred = values - jnp.mean(values, axis=-1, keepdims=True)
    scale = lax.rsqrt(jnp.mean(centred * centred, axis=-1, keepdims=True) + EPS_NORM)
    return centred * scale, scale


def norm_back(grad_xhat, xhat, scale):
    return scale * (
        grad_xhat
        - jnp.mean(grad_xhat, axis=-1, keepdims=True)
        - xhat * jnp.mean(grad_xhat * xhat, axis=-1, keepdims=True)
    )


def gelu_both(values):
    phi = 0.5 * (1.0 + lax.erf(values * math.sqrt(0.5)))
    bell = jnp.exp(-0.5 * values * values) * (1.0 / math.sqrt(2.0 * math.pi))
    return values * phi, phi + values * bell


def after(value, *first):
    return lax.optimization_barrier((value, first))[0]


SMEM = pl.BlockSpec(memory_space=pltpu.SMEM)


def fixed(array):
    shape = array.shape
    return pl.BlockSpec(
        shape, lambda *_: (0,) * len(shape), pipeline_mode=pl.Buffered(1)
    )


def run(kernel, cost, grid, ins, outs, scratch=()):
    return pl.pallas_call(
        kernel,
        grid=grid,
        in_specs=[spec for _, spec in ins],
        out_specs=[spec for _, _, spec in outs],
        out_shape=[jax.ShapeDtypeStruct(shape, kind) for shape, kind, _ in outs],
        scratch_shapes=list(scratch),
        compiler_params=pltpu.CompilerParams(vmem_limit_bytes=56 * 1024 * 1024),
        cost_estimate=pl.CostEstimate(
            flops=1024, bytes_accessed=int(COST_SCALE * cost), transcendentals=0
        ),
    )(*(array for array, _ in ins))


class Order:
    def __init__(self, where_ref, outer, block, quarter):
        self.rank, self.y = where_ref[0], where_ref[1]
        self.outer, self.block, self.quarter = outer, block, quarter

    def relative(self, k):
        start = (((k % 2) ^ self.y) * self.outer + k // 2) * self.block
        return pl.ds(pl.multiple_of(start, self.block), self.block)

    def natural(self, k):
        return slice(k * self.block, (k + 1) * self.block)

    def blocks(self):
        return range(2 * self.outer)

    def quarter_of(self, d):
        start = (self.rank ^ TURNS[d]) * self.quarter
        return pl.ds(pl.multiple_of(start, self.quarter), self.quarter)


def mixing_forward_kernel(
    order, where, h, w_mix, gain, bias, mixer, streams, normed, coef_out, pre_out
):
    order = order(where)
    hist_len, rows, width = h.shape
    step = 512
    xhat, _ = standardise(h[hist_len - 1].astype(F32))
    mix_normed = (xhat * gain[0:1, :]).astype(BF)
    pre = dot_nt(mix_normed, w_mix[...])
    hidden = gelu_both(pre)[0].astype(BF)
    coef = dot(hidden, mixer[...])
    pre_out[...] = pre
    coef_out[...] = coef
    for start in range(0, width, step):
        lanes = slice(start, start + step)
        parts = [h[j, :, lanes].astype(F32) for j in range(hist_len)]
        for a in range(4):
            first = a * hist_len
            total = coef[:, first : first + 1] * parts[0]
            for j in range(1, hist_len):
                total = total + coef[:, first + j : first + j + 1] * parts[j]
            streams[a, :, lanes] = total
    for a in range(3):
        xhat, _ = standardise(streams[a])
        low = (xhat * gain[1:2, :] + bias[0:1, :]).astype(BF)
        for k in order.blocks():
            normed[a, :, order.relative(k)] = low[:, order.natural(k)]


def turn(values, cos_table, sin_table):
    half_width = ROT // 2
    lane = lax.broadcasted_iota(jnp.int32, values.shape, 1)
    partner = jnp.where(
        lane < half_width,
        pltpu.roll(values, HD - half_width, axis=1),
        pltpu.roll(values, half_width, axis=1),
    )
    return values * cos_table + partner * sin_table


def head_scores(query, key):
    seq_len = query.shape[0]
    scores = dot_nt(query, key) * (1.0 / math.sqrt(HD))
    row = lax.broadcasted_iota(jnp.int32, (seq_len, seq_len), 0)
    column = lax.broadcasted_iota(jnp.int32, (seq_len, seq_len), 1)
    scores = jnp.where(row >= column, scores, NEGATIVE)
    exponent = jnp.exp(scores - jnp.max(scores, axis=-1, keepdims=True))
    return exponent / jnp.sum(exponent, axis=-1, keepdims=True)


def attention_forward_kernel(*refs):
    normed, (own, other, cos, sin) = refs[:4], refs[4:8]
    attended, query_rot, key_rot, value, made, held, arrived = refs[8:]
    quarter = attended.shape[1]
    half = own.shape[0]
    seq_len = cos.shape[0]
    copies = [
        pltpu.make_async_copy(normed[d], held.at[d], arrived.at[d]) for d in range(4)
    ]
    for copy in copies:
        copy.start()
    cos_table, sin_table = cos[...], sin[...]
    for d in range(4):
        copies[d].wait()
        rows = slice(d * seq_len, (d + 1) * seq_len)
        for a in range(3):
            lanes = slice(a * quarter, (a + 1) * quarter)
            made[a] = dot(held[d, a, :, :half], own[:, lanes]) + dot(
                held[d, a, :, half:], other[:, lanes]
            )
        value[rows, :] = made[2].astype(BF)
        for head in range(quarter // HD):
            lanes = slice(head * HD, (head + 1) * HD)
            query = turn(made[0, :, lanes], cos_table, sin_table).astype(BF)
            key = turn(made[1, :, lanes], cos_table, sin_table).astype(BF)
            query_rot[rows, lanes] = query
            key_rot[rows, lanes] = key
            probs = head_scores(query, key).astype(BF)
            attended[rows, lanes] = dot(probs, value[rows, lanes]).astype(BF)


def attention_backward_kernel(q, k, v, g, own, other, cos, sin, grads, *backs):
    quarter = q.shape[1]
    half = own.shape[0]
    scale = 1.0 / math.sqrt(HD)
    cos_table, sin_table = cos[...], -sin[...]
    for head in range(quarter // HD):
        lanes = slice(head * HD, (head + 1) * HD)
        query, key, grad = q[:, lanes], k[:, lanes], g[:, lanes]
        probs = head_scores(query, key)
        grad_probs = dot_nt(grad, v[:, lanes])
        centre = jnp.sum(probs * grad_probs, axis=-1, keepdims=True)
        grad_scores = (probs * (grad_probs - centre)).astype(BF)
        grads[0, :, lanes] = turn(dot(grad_scores, key) * scale, cos_table, sin_table).astype(BF)
        grads[1, :, lanes] = turn(
            dot_tn(grad_scores, query) * scale, cos_table, sin_table
        ).astype(BF)
        grads[2, :, lanes] = dot_tn(probs.astype(BF), grad).astype(BF)

    def send(outs):
        for a in range(3):
            columns = slice(a * quarter, (a + 1) * quarter)
            outs[a][:, :half] = dot_nt(grads[a], own[:, columns]).astype(BF)
            outs[a][:, half:] = dot_nt(grads[a], other[:, columns]).astype(BF)

    for step in range(2):
        outs = backs[3 * step : 3 * step + 3]
        pl.when(pl.program_id(0) == step)(functools.partial(send, outs))


def residual_kernel(order, where, *refs):
    order = order(where)
    parts, weights = refs[:4], refs[4:12]
    stream, gain, bias, residual, normed, attended, natural = refs[12:]
    half = weights[0].shape[0]
    for d in range(4):
        natural[:, order.quarter_of(d)] = parts[d][...]
    for k in order.blocks():
        attended[:, order.relative(k)] = natural[:, order.natural(k)]
    for d in range(4):
        columns = order.quarter_of(d)
        residual[:, columns] = (
            stream[0, :, columns]
            + dot(attended[:, :half], weights[2 * d][...])
            + dot(attended[:, half:], weights[2 * d + 1][...])
        )
    xhat, _ = standardise(residual[...])
    low = (xhat * gain[2:3, :] + bias[1:2, :]).astype(BF)
    for k in order.blocks():
        normed[:, order.relative(k)] = low[:, order.natural(k)]


def up_kernel(*refs):
    rows, (own, other, activated, slope) = refs[:4], refs[4:]
    half = own.shape[0]
    seq_len = rows[0].shape[0]
    for d in range(4):
        up = dot(rows[d][:, :half], own[...]) + dot(rows[d][:, half:], other[...])
        active, back = gelu_both(up)
        activated[d * seq_len : (d + 1) * seq_len, :] = active.astype(BF)
        slope[d * seq_len : (d + 1) * seq_len, :] = back


def down_grad_kernel(activated, *refs):
    rows, out = refs[:4], refs[4]
    seq_len = rows[0].shape[0]
    total = dot_tn(activated[:seq_len, :], rows[0][...])
    for d in range(1, 4):
        total = total + dot_tn(activated[d * seq_len : (d + 1) * seq_len, :], rows[d][...])
    out[...] = total.astype(BF)


def hidden_back_kernel(*refs):
    rows, (weight, slope, out) = refs[:4], refs[4:]
    seq_len = rows[0].shape[0]
    for d in range(4):
        part = slice(d * seq_len, (d + 1) * seq_len)
        out[part, :] = (dot_nt(rows[d][...], weight[...]) * slope[part, :]).astype(BF)


def down_kernel(activated, weight, *outs):
    total = dot(activated[...], weight[...]).astype(BF)
    seq_len = outs[0].shape[0]
    for d in range(4):
        outs[d][...] = total[d * seq_len : (d + 1) * seq_len]


def up_grad_kernel(*refs):
    rows, (grad, out) = refs[:4], refs[4:]
    seq_len = rows[0].shape[0]
    total = dot_tn(rows[0][...], grad[:seq_len, :])
    for d in range(1, 4):
        total = total + dot_tn(rows[d][...], grad[d * seq_len : (d + 1) * seq_len, :])
    out[...] = total.astype(BF)


def normed_back_kernel(pair, grad, own, other, *outs):
    step, steps = pl.program_id(0), pl.num_programs(0)
    seq_len = outs[0].shape[0]

    def send(weight):
        for d, out in zip(pair, outs):
            rows = slice(d * seq_len, (d + 1) * seq_len)
            out[...] = dot_nt(grad[rows, :], weight[...]).astype(BF)

    pl.when(step < steps // 2)(functools.partial(send, own))
    pl.when(step >= steps // 2)(functools.partial(send, other))


def residual_back_kernel(order, where, *refs):
    order = order(where)
    residual, gain, mine, from_core, from_x, grad_out = refs[:6]
    weights = refs[6:14]
    grad, grad_gain, grad_bias = refs[14:17]
    parts, wide, low = refs[17:21], refs[21], refs[22]
    half = weights[0].shape[0]
    for k in order.blocks():
        source = order.relative(k)
        wide[:, order.natural(k)] = (
            mine[:, source].astype(F32)
            + from_core[:, source].astype(F32)
            + from_x[:, source].astype(F32)
        )
    xhat, scale = standardise(residual[...])
    grad_y = wide[...]
    grad_gain[...] = jnp.sum(grad_y * xhat, axis=0, keepdims=True)
    grad_bias[...] = jnp.sum(grad_y, axis=0, keepdims=True)
    grad_x = norm_back(grad_y * gain[2:3, :], xhat, scale)
    grad[...] = (grad_out[...].astype(F32) + grad_x).astype(BF)
    for s in range(2):
        total = dot_nt(grad[:, order.quarter_of(0)], weights[s][...])
        for d in range(1, 4):
            total = total + dot_nt(grad[:, order.quarter_of(d)], weights[2 * d + s][...])
        low[:, s * half : (s + 1) * half] = total.astype(BF)
    for k in order.blocks():
        wide[:, order.natural(k)] = low[:, order.relative(k)].astype(F32)
    for d in range(4):
        parts[d][...] = wide[:, order.quarter_of(d)].astype(BF)


def out_grad_kernel(order, where, attended, grad, *outs):
    order = order(where)
    for d in range(4):
        outs[d][...] = dot_tn(attended[...], grad[:, order.quarter_of(d)]).astype(BF)


def in_grad_kernel(*refs):
    normed, (even, odd, out) = refs[:4], refs[4:]
    seq_len = normed[0].shape[1]
    total = None
    for d in range(4):
        rows = slice(d // 2 * seq_len, (d // 2 + 1) * seq_len)
        part = dot_tn(normed[d][0], (odd if d % 2 else even)[0, rows, :])
        total = part if total is None else total + part
    out[...] = total.astype(BF)


def mixing_backward_kernel(order, where, *refs):
    order = order(where)
    h, streams, coef_in, pre_in = refs[:4]
    mine, from_core, from_x = refs[4:7], refs[7:10], refs[10]
    grad_residual, w_mix, gain, mixer = refs[11:15]
    grad_history, grad_mix, grad_mixer, grad_gains, grad_bias = refs[15:20]
    grad_streams = refs[20]
    hist_len, rows, width = h.shape
    step = 512

    @pl.when(pl.program_id(0) == 0)
    def _():
        grad_mix[...] = jnp.zeros_like(grad_mix)
        grad_mixer[...] = jnp.zeros_like(grad_mixer)
        grad_gains[...] = jnp.zeros_like(grad_gains)
        grad_bias[...] = jnp.zeros_like(grad_bias)

    for a in range(3):
        for k in order.blocks():
            source = order.relative(k)
            grad_streams[a, :, order.natural(k)] = (
                mine[a][:, source].astype(F32)
                + from_core[a][:, source].astype(F32)
                + from_x[a, :, source].astype(F32)
            )
        xhat, scale = standardise(streams[a])
        grad_y = grad_streams[a]
        grad_gains[1:2, :] += jnp.sum(grad_y * xhat, axis=0, keepdims=True)
        grad_bias[...] += jnp.sum(grad_y, axis=0, keepdims=True)
        grad_streams[a] = norm_back(grad_y * gain[1:2, :], xhat, scale)
    grad_streams[3] = grad_residual[...].astype(F32)

    coef = coef_in[...]
    columns = coef.shape[1]
    sums = [jnp.zeros((rows, 128), F32) for _ in range(columns)]
    for start in range(0, width, step):
        lanes = slice(start, start + step)
        grads = [grad_streams[a, :, lanes] for a in range(4)]
        for j in range(hist_len):
            part = h[j, :, lanes].astype(F32)
            back = coef[:, j : j + 1] * grads[0]
            for a in range(1, 4):
                at = a * hist_len + j
                back = back + coef[:, at : at + 1] * grads[a]
            for a in range(4):
                product = grads[a] * part
                folded = product[:, 0:128]
                for lane in range(128, step, 128):
                    folded = folded + product[:, lane : lane + 128]
                sums[a * hist_len + j] = sums[a * hist_len + j] + folded
            if j < hist_len - 1:
                grad_history[j, :, lanes] = back.astype(BF)
            else:
                grad_streams[3, :, lanes] = back
    lane = lax.broadcasted_iota(jnp.int32, (rows, columns), 1)
    grad_coef = jnp.zeros((rows, columns), F32)
    for at in range(columns):
        grad_coef = jnp.where(lane == at, jnp.sum(sums[at], axis=-1, keepdims=True), grad_coef)
    grad_coef = grad_coef.astype(BF)
    hidden, slope = gelu_both(pre_in[...])
    hidden = hidden.astype(BF)
    grad_mixer[...] += dot_tn(hidden, grad_coef)
    grad_pre = (dot_nt(grad_coef, mixer[...]) * slope).astype(BF)
    xhat, scale = standardise(h[hist_len - 1].astype(F32))
    grad_mix[...] += dot_tn(grad_pre, (xhat * gain[0:1, :]).astype(BF))
    grad_y = dot(grad_pre, w_mix[...])
    grad_gains[0:1, :] += jnp.sum(grad_y * xhat, axis=0, keepdims=True)
    grad_current = norm_back(grad_y * gain[0:1, :], xhat, scale)
    grad_history[hist_len - 1] = (grad_streams[3] + grad_current).astype(BF)


def rotary_tables(seq_len):
    half_width = ROT // 2
    frequency = 10000.0 ** (-(2.0 * jnp.arange(half_width, dtype=F32)) / ROT)
    angles = jnp.arange(seq_len, dtype=F32)[:, None] * frequency[None, :]
    cosine, sine = jnp.cos(angles), jnp.sin(angles)
    rest = HD - ROT
    cos_table = jnp.concatenate([cosine, cosine, jnp.ones((seq_len, rest), F32)], axis=1)
    sin_table = jnp.concatenate([-sine, sine, jnp.zeros((seq_len, rest), F32)], axis=1)
    return cos_table, sin_table


def place_kernel(order, where, *refs):
    order = order(where)
    parts, (weight_in, weight_out) = refs[:4], refs[4:]
    quarter = order.quarter
    for d in range(4):
        for a in range(4):
            start = (a % 3) * 4 * quarter + (order.rank ^ TURNS[d]) * quarter
            lanes = pl.ds(pl.multiple_of(start, quarter), quarter)
            target = weight_out if a == 3 else weight_in
            if a == 3:
                lanes = order.quarter_of(d)
            target[:, lanes] = parts[d][:, a * quarter : (a + 1) * quarter]


def moments_kernel(share, clip_ref, *refs):
    clip = clip_ref[0]
    step = 512

    @pl.when(pl.program_id(0) == 0)
    def _():
        for member in range(4):
            refs[26][member] = 0.0
        refs[26][4] = jnp.sum(refs[16][...] * refs[16][...])
        refs[26][5] = jnp.sum(refs[17][...] * refs[17][...]) * share

    for member in range(4):
        grad, first, second, weight = refs[4 * member : 4 * member + 4]
        first_out, second_out = refs[18 + 2 * member : 20 + 2 * member]
        total = 0.0
        for start in range(0, grad.shape[1], step):
            lanes = slice(start, start + step)
            scaled = grad[:, lanes].astype(F32) * clip
            first_new = BETA * first[:, lanes] + (1.0 - BETA) * scaled
            second_new = BETA * second[:, lanes] + (1.0 - BETA) * scaled * scaled
            first_out[:, lanes] = first_new
            second_out[:, lanes] = second_new
            change = first_new / (jnp.sqrt(second_new) + EPS_ADAM) + DECAY_WEIGHT * weight[:, lanes]
            total = total + jnp.sum(change * change, axis=0, keepdims=True)
        refs[26][member] = refs[26][member] + jnp.sum(total)


def apply_kernel(trust_ref, *refs):
    step = 512
    for member in range(4):
        first, second, weight = refs[3 * member : 3 * member + 3]
        out, low = refs[20 + 2 * member : 22 + 2 * member]
        rate = RATE_MATRIX * trust_ref[member]
        for start in range(0, weight.shape[1], step):
            lanes = slice(start, start + step)
            old = weight[:, lanes]
            change = first[:, lanes] / (jnp.sqrt(second[:, lanes]) + EPS_ADAM) + DECAY_WEIGHT * old
            new = old - rate * change
            out[:, lanes] = new
            low[:, lanes] = new.astype(BF)

    @pl.when(pl.program_id(0) == 0)
    def _():
        for member in range(4):
            change, weight = refs[12 + 2 * member : 14 + 2 * member]
            out, low = refs[28 + 2 * member : 30 + 2 * member]
            rate = RATE_MATRIX * trust_ref[4 + member] if member < 2 else RATE_VECTOR
            new = weight[...] - rate * change[...]
            out[...] = new
            low[...] = new.astype(BF)


class Links:
    def __init__(self, devices, width):
        self.devices = devices
        index = lax.axis_index("dp")
        self.core = index & 1
        self.x = (index >> 1) & 1
        self.rank = index & 3
        self.index = index
        self.y_bit = 2
        self.block = 4 * width // devices
        while self.block % 128:
            self.y_bit += 1
            self.block *= 2
        self.inner = 1 << (self.y_bit - 2)
        self.outer = width // (2 * self.block)
        self.y = (index >> self.y_bit) & 1
        self.where = jnp.stack([self.rank, self.y]).astype(jnp.int32)
        groups = {}
        for j in range(devices):
            groups.setdefault((j & 3, (j >> self.y_bit) & 1), []).append(j)
        self.z_groups = list(groups.values())

    def swap(self, value, bit):
        return lax.ppermute(value, "dp", [(j, j ^ bit) for j in range(self.devices)])

    def swap_core(self, value):
        return self.swap(value, 1)

    def swap_x(self, value):
        return self.swap(value, 2)

    def swap_y(self, value):
        return self.swap(value, 1 << self.y_bit)

    def gather(self, value, groups):
        return lax.all_gather(value, "dp", axis=0, tiled=True, axis_index_groups=groups)

    def reduce(self, value, groups):
        return lax.psum_scatter(
            value, "dp", scatter_dimension=0, tiled=True, axis_index_groups=groups
        )

    def total(self, value):
        bit = 1
        while bit < self.devices:
            pair = value + self.swap(value, bit)
            if 2 * bit < self.devices:
                pair = pair + (self.swap(value, 2 * bit) + self.swap(value, 3 * bit))
            value = pair
            bit *= 4
        return value

    def to_absolute(self, parts):
        own, across_x, across_core, across_both = parts
        low_x = self.x == 0
        core_own = (jnp.where(low_x, own, across_x), jnp.where(low_x, across_x, own))
        core_other = (
            jnp.where(low_x, across_core, across_both),
            jnp.where(low_x, across_both, across_core),
        )
        low_core = self.core == 0
        ordered = []
        for mine, other in zip(core_own, core_other):
            ordered.append(jnp.where(low_core, mine, other))
            ordered.append(jnp.where(low_core, other, mine))
        return ordered

    def to_relative(self, parts):
        low_x, low_core = self.x == 0, self.core == 0
        near = [jnp.where(low_x, parts[c], parts[2 + c]) for c in (0, 1)]
        far = [jnp.where(low_x, parts[2 + c], parts[c]) for c in (0, 1)]
        return [
            jnp.where(low_core, near[0], near[1]),
            jnp.where(low_core, far[0], far[1]),
            jnp.where(low_core, near[1], near[0]),
            jnp.where(low_core, far[1], far[0]),
        ]

    def group_gather(self, value):
        across_x = self.swap_x(value)
        return [value, across_x, self.swap_core(value), self.swap_core(across_x)]

    def group_exchange(self, parts):
        own, *others = parts
        return [own] + [self.swap(part, turn) for part, turn in zip(others, TURNS[1:])]

    def group_reduce(self, own, for_x, for_core, for_both, *ties):
        from_both = self.swap_core(for_both)
        for_x = (for_x.astype(F32) + from_both.astype(F32)).astype(BF)
        return self.swap_core(for_core), self.swap_x(after(for_x, *ties)), for_x


def program(
    devices,
    history,
    d_out,
    group_ids,
    group_weight,
    attn_in,
    attn_out,
    ffn_up,
    ffn_down,
    mixer_in,
    mixer_out,
    norm_gain,
    norm_bias,
    first_attn_in,
    second_attn_in,
    first_attn_out,
    second_attn_out,
    first_ffn_up,
    second_ffn_up,
    first_ffn_down,
    second_ffn_down,
    first_mixer_in,
    second_mixer_in,
    first_mixer_out,
    second_mixer_out,
    first_norm_gain,
    second_norm_gain,
    first_norm_bias,
    second_norm_bias,
):
    hist_len, seq_len, width = history.shape
    links = Links(devices, width)
    order = functools.partial(
        Order, outer=links.outer, block=links.block, quarter=width // 4
    )
    with_order = lambda kernel: functools.partial(kernel, order)
    where = (links.where, SMEM)
    quarter, half = width // 4, width // 2
    rows = width // devices
    hidden = ffn_down.shape[0] * devices
    units = hidden // devices
    share = hidden // 4
    four = 4 * seq_len
    whole = lambda array: (array, fixed(array))

    low_attn = attn_in.astype(BF).reshape(rows, 3, 4, quarter)
    low_out = attn_out.astype(BF).reshape(rows, 1, 4, quarter)
    by_rank = jnp.concatenate([low_attn, low_out], axis=1)
    by_rank = [by_rank[:, :, r].reshape(rows, width) for r in range(4)]
    attn_parts = links.group_exchange(links.to_relative(by_rank))
    attn_block = jnp.concatenate(links.to_absolute(attn_parts), axis=0)

    low_up = ffn_up.astype(BF).reshape(rows, links.outer, 2, links.inner, 4, units)
    low_up = jnp.transpose(low_up, (4, 0, 1, 3, 2, 5)).reshape(4, rows, share)
    up_parts = after(links.to_relative(list(low_up)), attn_parts[1], attn_parts[3])
    up_parts = links.group_exchange(up_parts)
    up_block = jnp.concatenate(links.to_absolute(up_parts), axis=0)

    low_down = ffn_down.astype(BF)
    other_down = links.swap_y(low_down)
    low_y = links.y == 0

    attn_own = links.gather(attn_block, links.z_groups)
    attn_other = links.swap_y(attn_own)
    up_own = links.gather(up_block, links.z_groups)
    up_other = links.swap_y(up_own)

    hidden_mix = mixer_in.shape[1]
    pack = jnp.concatenate([mixer_in.T, norm_gain, norm_bias], axis=0).astype(BF)
    bit = 1
    while bit < devices:
        other = links.swap(pack, bit)
        low = (links.index & bit) == 0
        pack = jnp.concatenate([jnp.where(low, pack, other), jnp.where(low, other, pack)], axis=1)
        bit *= 2
    w_mixer_in = pack[:hidden_mix]
    gain_table = pack[hidden_mix : hidden_mix + 3].astype(F32)
    bias_table = pack[hidden_mix + 3 :].astype(F32)
    mixer_low = mixer_out.astype(BF)

    tile = 64
    steps = (seq_len // tile,)
    columns = mixer_out.shape[1]
    row_tile = lambda *lead: pl.BlockSpec(
        lead + (tile, width), lambda t: (0,) * len(lead) + (t, 0)
    )
    narrow = pl.BlockSpec((tile, columns), lambda t: (t, 0))
    pre_narrow = pl.BlockSpec((tile, hidden_mix), lambda t: (t, 0))
    streams, normed, coef, mix_pre = run(
        with_order(mixing_forward_kernel),
        14,
        steps,
        [
            where,
            (history, row_tile(hist_len)),
            whole(w_mixer_in),
            whole(gain_table),
            whole(bias_table),
            whole(mixer_low),
        ],
        [
            ((4, seq_len, width), F32, row_tile(4)),
            ((3, seq_len, width), BF, row_tile(3)),
            ((seq_len, columns), F32, narrow),
            ((seq_len, hidden_mix), F32, pre_narrow),
        ],
    )

    low_down, other_down = after((low_down, other_down), normed)
    down_block = jnp.concatenate(
        [jnp.where(low_y, low_down, other_down), jnp.where(low_y, other_down, low_down)], axis=0
    )
    w_down = links.gather(down_block, links.z_groups)

    tables = [whole(table) for table in rotary_tables(seq_len)]
    normed_four = links.group_gather(normed)
    attn_weights = [
        (
            array,
            pl.BlockSpec((half, 3 * quarter), lambda s: (0, 0), pipeline_mode=pl.Buffered(1)),
        )
        for array in (attn_own, attn_other)
    ]
    out_mine = [array[:, 3 * quarter :] for array in (attn_own, attn_other)]
    out_x = [links.swap_x(array) for array in out_mine]
    group_count = group_weight.shape[0]
    seq_weight = jnp.sum(
        jnp.where(jnp.arange(group_count, dtype=jnp.int32) == group_ids[0], group_weight, 0.0)
    )
    grad_out = (d_out.astype(F32) * seq_weight).astype(BF)
    grad_out = after(grad_out, normed_four[1])
    grad_out_x = links.swap_x(grad_out)
    seq_block = pl.BlockSpec((seq_len, quarter), lambda s: (s, 0))
    attn_other_now = after(attn_other, grad_out_x)
    anywhere = pl.BlockSpec(memory_space=pl.ANY)
    four_quarter = pl.BlockSpec((four, quarter), lambda _: (0, 0))
    attended, query_rot, key_rot, value = run(
        attention_forward_kernel,
        16,
        (1,),
        [(part, anywhere) for part in normed_four]
        + [(attn_own, attn_weights[0][1]), (attn_other_now, attn_weights[0][1])]
        + tables,
        [((four, quarter), BF, four_quarter)] * 4,
        [
            pltpu.VMEM((3, seq_len, quarter), F32),
            pltpu.VMEM((4, 3, seq_len, width), BF),
            pltpu.SemaphoreType.DMA((4,)),
        ],
    )
    out_x = after(out_x, attended)
    out_halves = [
        [out_mine[k], out_x[k], links.swap_core(out_mine[k]), links.swap_core(out_x[k])]
        for k in range(2)
    ]
    w_out = [out_halves[k][d] for d in range(4) for k in range(2)]
    attended = links.group_exchange(
        [attended[d * seq_len : (d + 1) * seq_len] for d in range(4)]
    )
    one_row = ((1, width), F32, pl.BlockSpec((1, width), lambda *_: (0, 0)))
    full = lambda kind: (
        (seq_len, width),
        kind,
        pl.BlockSpec((seq_len, width), lambda *_: (0, 0)),
    )
    residual, ffn_normed, attended_rel = run(
        with_order(residual_kernel),
        9,
        (1,),
        [where]
        + [whole(part) for part in attended]
        + [whole(part) for part in w_out]
        + [
            (
                streams,
                pl.BlockSpec(
                    (1, seq_len, width), lambda _: (3, 0, 0), pipeline_mode=pl.Buffered(1)
                ),
            ),
            whole(gain_table),
            whole(bias_table),
        ],
        [full(F32), full(BF), full(BF)],
        [pltpu.VMEM((seq_len, width), BF)],
    )

    ffn_four = links.group_gather(ffn_normed)
    wide = 256
    column_tile = lambda count: pl.BlockSpec((count, wide), lambda t: (0, t))
    line_tile = lambda count: pl.BlockSpec((wide, count), lambda t: (t, 0))
    activated, slope = run(
        up_kernel,
        17,
        (share // wide,),
        [whole(part) for part in ffn_four]
        + [(up_own, column_tile(half)), (up_other, column_tile(half))],
        [((four, share), BF, column_tile(four)), ((four, share), F32, column_tile(four))],
    )

    grad_out_x = after(grad_out_x, activated)
    grad_out_four = [
        grad_out,
        grad_out_x,
        links.swap_core(grad_out),
        links.swap_core(grad_out_x),
    ]

    (grad_down,) = run(
        down_grad_kernel,
        14,
        (share // wide,),
        [(activated, column_tile(four))] + [whole(part) for part in grad_out_four],
        [((share, width), BF, line_tile(width))],
    )
    down_sums = links.reduce(grad_down, links.z_groups)

    (grad_up,) = run(
        hidden_back_kernel,
        16,
        (share // wide,),
        [whole(part) for part in grad_out_four]
        + [(w_down, line_tile(width)), (after(slope, grad_down), column_tile(four))],
        [((four, share), BF, column_tile(four))],
    )

    def rows_of_four(block):
        parts = list(block.reshape(4, rows, block.shape[1]))
        return links.group_exchange(links.to_relative(parts))

    def whole_rows(parts):
        return jnp.stack(links.to_absolute(parts), axis=1)

    tiles = half // wide

    def normed_back(pair, grad):
        return run(
            functools.partial(normed_back_kernel, pair),
            11,
            (2 * tiles,),
            [
                whole(grad),
                (up_own, pl.BlockSpec((wide, share), lambda t: (jnp.minimum(t, tiles - 1), 0))),
                (up_other, pl.BlockSpec((wide, share), lambda t: (jnp.maximum(t - tiles, 0), 0))),
            ],
            [((seq_len, width), BF, column_tile(seq_len))] * 2,
        )

    def up_grad(first, count, grad):
        block = pl.BlockSpec((seq_len, wide), lambda t: (0, first + t))
        (out,) = run(
            up_grad_kernel,
            9,
            (count,),
            [(part, block) for part in ffn_four] + [whole(grad)],
            [((count * wide, share), BF, line_tile(share))],
        )
        return out

    for_x, for_both = normed_back((1, 3), grad_up)
    up_first = up_grad(tiles, 1, after(grad_up, for_both))
    up_theirs_first = links.swap_y(up_first)
    up_second = up_grad(tiles + 1, 1, after(grad_up, up_first))
    up_theirs_second = links.swap_y(up_second)
    up_rest = up_grad(tiles + 2, tiles - 2, after(grad_up, up_second))
    up_theirs_rest = links.swap_y(up_rest)
    own, for_core = normed_back((0, 2), after(grad_up, up_rest))
    up_grad_own = up_grad(0, tiles, after(grad_up, own))
    from_core, from_x, _ = links.group_reduce(own, for_x, for_core, for_both)
    from_x = after(from_x, up_grad_own, up_theirs_first)
    part_out = ((seq_len, quarter), BF, pl.BlockSpec((seq_len, quarter), lambda _: (0, 0)))
    back = run(
        with_order(residual_back_kernel),
        11,
        (1,),
        [
            where,
            whole(residual),
            whole(gain_table),
            whole(own),
            whole(from_core),
            whole(from_x),
            whole(grad_out),
        ]
        + [whole(part) for part in w_out],
        [full(BF), one_row, one_row] + [part_out] * 4,
        [pltpu.VMEM((seq_len, width), F32), pltpu.VMEM((seq_len, width), BF)],
    )
    grad_residual, grad_gain_ffn, grad_bias_ffn = back[:3]

    grad_heads = links.group_exchange(back[3:])

    line = 512
    out_parts = run(
        with_order(out_grad_kernel),
        7,
        (width // line,),
        [
            where,
            (attended_rel, pl.BlockSpec((seq_len, line), lambda t: (0, t))),
            whole(grad_residual),
        ],
        [((width, quarter), BF, pl.BlockSpec((line, quarter), lambda t: (t, 0)))] * 4,
    )
    out_parts = after(out_parts, grad_heads[1], grad_heads[3])
    out_both = [links.swap_core(out_parts[3][k * half : (k + 1) * half]) for k in range(2)]
    out_core = links.swap_core(out_parts[2])

    def attention_back(first, *ties):
        heads = jnp.concatenate([grad_heads[first], grad_heads[first + 2]], axis=0)
        block = pl.BlockSpec((seq_len, quarter), lambda s: (first + 2 * s, 0))
        proj, *backs = run(
            attention_backward_kernel,
            15,
            (2,),
            [(query_rot, block), (key_rot, block), (value, block)]
            + [(after(heads, *ties), seq_block)]
            + attn_weights
            + tables,
            [
                (
                    (3, 2 * seq_len, quarter),
                    BF,
                    pl.BlockSpec((3, seq_len, quarter), lambda s: (0, s, 0)),
                )
            ]
            + [full(BF)] * 6,
        )
        return proj, backs[:3], backs[3:]

    plus = lambda mine, theirs: (mine.astype(F32) + theirs.astype(F32)).astype(BF)
    proj_odd, for_x, for_both = attention_back(1, up_theirs_second)
    out_both = after(out_both, for_both)
    out_for_x = [plus(out_parts[1][k * half : (k + 1) * half], out_both[k]) for k in range(2)]
    out_x_other = links.swap_x(out_for_x[1])
    out_x_own = links.swap_x(out_for_x[0])
    proj_even, own, for_core = attention_back(0, out_for_x)
    back_own = own
    from_both = [links.swap_core(part) for part in for_both]
    back_core = [links.swap_core(part) for part in for_core]
    for_x = jnp.stack([plus(part, other) for part, other in zip(for_x, from_both)])
    back_x = links.swap_x(for_x)
    proj_even = after(proj_even, for_x)

    def in_grad(s, proj):
        block = pl.BlockSpec((1, seq_len, wide), lambda a, t: (a, 0, s * tiles + t))
        proj_block = pl.BlockSpec((1, 2 * seq_len, quarter), lambda a, t: (a, 0, 0))
        (out,) = run(
            in_grad_kernel,
            12,
            (3, tiles),
            [(part, block) for part in normed_four] + [(proj, proj_block), (proj_odd, proj_block)],
            [((half, 3 * quarter), BF, pl.BlockSpec((wide, quarter), lambda a, t: (t, a)))],
        )
        return out

    in_grad_other = in_grad(1, proj_even)
    in_theirs = links.swap_y(in_grad_other)
    in_grad_own = in_grad(0, after(proj_even, in_grad_other))

    up_theirs = jnp.concatenate(
        [up_theirs_first, up_theirs_second, after(up_theirs_rest, in_grad_own, out_x_other)]
    )
    up_both = after(plus(up_grad_own, up_theirs), down_sums)
    up_sums = links.reduce(up_both, links.z_groups)
    three = lambda k, theirs: (
        out_parts[0][k * half : (k + 1) * half].astype(F32)
        + out_core[k * half : (k + 1) * half].astype(F32)
        + theirs.astype(F32)
    )
    out_theirs = links.swap_y(three(1, after(out_x_other, up_both)).astype(BF))

    down_parts = run(
        down_kernel,
        14,
        (width // wide,),
        [whole(after(activated, up_both)), (w_down, column_tile(share))],
        [((seq_len, width), BF, column_tile(seq_len))] * 4,
    )
    down_core = links.swap_core(down_parts[2])
    down_for_x = plus(down_parts[1], links.swap_core(down_parts[3]))

    weights = (attn_in, attn_out, ffn_up, ffn_down, mixer_in, mixer_out, norm_gain, norm_bias)
    square = lambda array: jnp.sum(jnp.square(array.astype(F32)))

    def portion(member, amount):
        return amount / devices if member == 5 else amount


    in_theirs = after(in_theirs, down_for_x)
    attn_both = jnp.concatenate(
        [plus(in_grad_own, in_theirs), plus(three(0, out_x_own), out_theirs)], axis=1
    )
    attn_both = after(attn_both, up_sums, back_x, back_core)
    up_four = rows_of_four(after(up_sums, attn_both))
    attn_sums = links.reduce(attn_both, links.z_groups)


    fixed_out = lambda shape: (
        shape,
        F32,
        pl.BlockSpec(shape, lambda t: (0, 0)),
    )
    grad_history, grad_mixer_in, grad_mixer_out, grad_gains, grad_bias_attn = run(
        with_order(mixing_backward_kernel),
        450,
        steps,
        [
            where,
            (history, row_tile(hist_len)),
            (streams, row_tile(3)),
            (coef, narrow),
            (mix_pre, pre_narrow),
        ]
        + [(part, row_tile()) for part in (*back_own, *back_core)]
        + [
            (back_x, row_tile(3)),
            (after(grad_residual, attn_both), row_tile()),
            whole(w_mixer_in),
            whole(gain_table),
            whole(mixer_low),
        ],
        [
            ((hist_len, seq_len, width), BF, row_tile(hist_len)),
            fixed_out((hidden_mix, width)),
            fixed_out((hidden_mix, columns)),
            fixed_out((2, width)),
            fixed_out((1, width)),
        ],
        [pltpu.VMEM((4, tile, width), F32)],
    )

    shard_up = jnp.transpose(
        whole_rows(up_four).reshape(rows, 4, links.outer, links.inner, 2, units),
        (0, 2, 4, 3, 1, 5),
    ).reshape(rows, hidden)

    down_x = links.swap_x(after(down_for_x, grad_gains))
    small = jnp.concatenate(
        [grad_mixer_in, grad_gains, grad_gain_ffn, grad_bias_attn, grad_bias_ffn], axis=0
    )
    top = devices.bit_length() - 2
    inner = 1 << (links.y_bit - 2)
    pieces = small.reshape(small.shape[0], devices // (8 * inner), 2, inner * 4 * rows)
    take = lambda array, at, axis: lax.dynamic_index_in_dim(array, at, axis, keepdims=False)
    pieces = take(pieces, links.y, 2) + links.swap_y(take(pieces, 1 - links.y, 2))
    down_sums = after(down_sums, pieces)
    down_sums = down_sums.reshape(2, units, width)
    down_mine = jnp.where(low_y, down_sums[0], down_sums[1])
    down_theirs = jnp.where(low_y, down_sums[1], down_sums[0])
    down_theirs = links.swap_y(down_theirs)
    shard_down = down_mine.astype(F32) + down_theirs.astype(F32)
    bits = [k for k in range(top, 1, -1) if k != links.y_bit]
    while bits:
        pair, bits = bits[:2], bits[2:]
        pieces = pieces.reshape(small.shape[0], 1 << len(pair), -1)
        at = sum(((links.index >> k) & 1) << e for e, k in enumerate(reversed(pair)))
        total = take(pieces, at, 1)
        for turn in range(1, 1 << len(pair)):
            mask = sum(((turn >> e) & 1) << k for e, k in enumerate(reversed(pair)))
            total = total + links.swap(take(pieces, at ^ turn, 1), mask)
        pieces = total
    pieces = after(pieces, down_theirs).reshape(small.shape[0], 4, rows)
    small = take(pieces, links.rank, 1)
    for turn in TURNS[1:]:
        small = small + links.swap(take(pieces, links.rank ^ turn, 1), turn)
    mixer_grad = links.total(grad_mixer_out)
    early_squares = square(up_sums) + square(shard_down) + square(small)
    early_squares = early_squares + square(mixer_grad) / devices
    attn_sums = after(attn_sums, shard_up, shard_down)
    block_of = lambda array_shape: pl.BlockSpec(array_shape, lambda t: (0, 0))
    shard_in, shard_out = run(
        with_order(place_kernel),
        PLACE_COST,
        (1,),
        [where] + [whole(part) for part in rows_of_four(attn_sums)],
        [
            ((rows, 3 * width), BF, block_of((rows, 3 * width))),
            ((rows, width), BF, block_of((rows, width))),
        ],
    )

    grads = (
        shard_in,
        shard_out,
        shard_up,
        shard_down,
        small[:hidden_mix].T,
        mixer_grad,
        small[hidden_mix : hidden_mix + 3],
        small[hidden_mix + 3 :],
    )

    firsts = (
        first_attn_in,
        first_attn_out,
        first_ffn_up,
        first_ffn_down,
        first_mixer_in,
        first_mixer_out,
        first_norm_gain,
        first_norm_bias,
    )
    seconds = (
        second_attn_in,
        second_attn_out,
        second_ffn_up,
        second_ffn_down,
        second_mixer_in,
        second_mixer_out,
        second_norm_gain,
        second_norm_bias,
    )

    local_squares = early_squares + square(attn_sums)
    weights_later = after(weights, coef)
    local_weight_sq = [portion(member, square(weights_later[member])) for member in range(6)]
    sums = links.total(jnp.stack([local_squares] + local_weight_sq))
    squares, weight_sq = sums[0], sums[1:]
    global_norm = jnp.sqrt(squares)
    clip = 0.3 * math.sqrt(PARAMS) / (global_norm + 1e-06)
    parts = rows // 16
    slab = lambda array: pl.BlockSpec(
        (array.shape[0] // parts, array.shape[1]), lambda t: (t, 0)
    )
    slabs = lambda *arrays: [(array, slab(array)) for array in arrays]
    made = lambda array, kind: (array.shape, kind, slab(array))
    ins, outs = [(clip[None], SMEM)], []
    for member in range(4):
        ins += slabs(grads[member], firsts[member], seconds[member], weights[member])
        outs += [made(weights[member], F32)] * 2
    outs.append(((6,), F32, SMEM))
    small_new, steps_small = [], []
    for member in range(4, 8):
        scaled = grads[member] * clip
        first_new = BETA * firsts[member] + (1.0 - BETA) * scaled
        second_new = BETA * seconds[member] + (1.0 - BETA) * scaled * scaled
        step_value = first_new / (jnp.sqrt(second_new) + EPS_ADAM)
        if member < 6:
            step_value = step_value + DECAY_WEIGHT * weights[member]
        small_new.append((first_new, second_new))
        steps_small.append(step_value)
    ins += [whole(steps_small[0]), whole(steps_small[1])]
    moments = run(
        functools.partial(moments_kernel, 1.0 / devices), 14, (parts,), ins, outs
    )
    down_x = after(down_x, moments[8])
    out_state = (
        residual + down_parts[0].astype(F32) + down_core.astype(F32) + down_x.astype(F32)
    ).astype(BF)

    firsts_new = list(moments[0:8:2]) + [first for first, _ in small_new]
    seconds_new = list(moments[1:8:2]) + [second for _, second in small_new]
    update_sq = links.total(moments[8])
    weight_norm = jnp.sqrt(weight_sq)
    update_norm = jnp.sqrt(update_sq)
    trust = weight_norm / (update_norm + 1e-06)
    lamb_stats = jnp.stack([weight_norm, update_norm, trust], axis=1)
    ins, outs = [(trust, SMEM)], []
    for member in range(4):
        ins += slabs(firsts_new[member], seconds_new[member], weights[member])
        outs += [made(weights[member], F32), made(weights[member], BF)]
    for member in range(4, 8):
        shape = weights[member].shape
        spec = pl.BlockSpec(shape, lambda t: (0, 0))
        ins += [(steps_small[member - 4], spec), (weights[member], spec)]
        outs += [(shape, F32, spec), (shape, BF, spec)]
    applied = run(apply_kernel, 10, (parts,), ins, outs)
    results = []
    for member in range(8):
        results += [*applied[2 * member : 2 * member + 2], firsts_new[member], seconds_new[member]]
    return (out_state, grad_history, global_norm, lamb_stats, *results)


def solution(mesh):
    rows, columns, whole = P("dp", None), P(None, "dp"), P()
    middle = P(None, "dp", None)
    matrices = (rows,) * 5 + (whole,) + (columns,) * 2
    moments = tuple(spec for spec in matrices for _ in range(2))
    results = tuple(spec for spec in matrices for _ in range(4))
    return jax.shard_map(
        functools.partial(program, mesh.shape["dp"]),
        mesh=mesh,
        in_specs=(middle, rows, P("dp"), whole) + matrices + moments,
        out_specs=(rows, middle, whole, whole) + results,
        check_vma=False,
    )
```

```python
import functools
import math

import jax
import jax.numpy as jnp
from jax import lax
from jax.experimental import pallas as pl
from jax.experimental.pallas import tpu as pltpu
from jax.sharding import PartitionSpec as P

HD = 128
ROT = 32
PARAMS = 50416912

EPS_NORM = 1e-05
EPS_ADAM = 1e-06
DECAY_WEIGHT = 0.01
RATE_MATRIX = 0.3
RATE_VECTOR = 0.25
BETA = 0.5
NEGATIVE = -1e30
COST_SCALE = 200e3
PLACE_COST = 450

BF = jnp.bfloat16
F32 = jnp.float32
TURNS = (0, 2, 1, 3)


def dot(left, right):
    return jnp.dot(left, right, preferred_element_type=F32)


def dot_tn(left, right):
    return lax.dot_general(left, right, (((0,), (0,)), ((), ())), preferred_element_type=F32)


def dot_nt(left, right):
    return lax.dot_general(left, right, (((1,), (1,)), ((), ())), preferred_element_type=F32)


def standardise(values):
    centred = values - jnp.mean(values, axis=-1, keepdims=True)
    scale = lax.rsqrt(jnp.mean(centred * centred, axis=-1, keepdims=True) + EPS_NORM)
    return centred * scale, scale


def norm_back(grad_xhat, xhat, scale):
    return scale * (
        grad_xhat
        - jnp.mean(grad_xhat, axis=-1, keepdims=True)
        - xhat * jnp.mean(grad_xhat * xhat, axis=-1, keepdims=True)
    )


def gelu_both(values):
    phi = 0.5 * (1.0 + lax.erf(values * math.sqrt(0.5)))
    bell = jnp.exp(-0.5 * values * values) * (1.0 / math.sqrt(2.0 * math.pi))
    return values * phi, phi + values * bell


def after(value, *first):
    return lax.optimization_barrier((value, first))[0]


SMEM = pl.BlockSpec(memory_space=pltpu.SMEM)


def fixed(array):
    shape = array.shape
    return pl.BlockSpec(
        shape, lambda *_: (0,) * len(shape), pipeline_mode=pl.Buffered(1)
    )


def run(kernel, cost, grid, ins, outs, scratch=()):
    return pl.pallas_call(
        kernel,
        grid=grid,
        in_specs=[spec for _, spec in ins],
        out_specs=[spec for _, _, spec in outs],
        out_shape=[jax.ShapeDtypeStruct(shape, kind) for shape, kind, _ in outs],
        scratch_shapes=list(scratch),
        compiler_params=pltpu.CompilerParams(vmem_limit_bytes=56 * 1024 * 1024),
        cost_estimate=pl.CostEstimate(
            flops=1024, bytes_accessed=int(COST_SCALE * cost), transcendentals=0
        ),
    )(*(array for array, _ in ins))


class Order:
    def __init__(self, where_ref, outer, block, quarter):
        self.rank, self.y = where_ref[0], where_ref[1]
        self.outer, self.block, self.quarter = outer, block, quarter

    def relative(self, k):
        start = (((k % 2) ^ self.y) * self.outer + k // 2) * self.block
        return pl.ds(pl.multiple_of(start, self.block), self.block)

    def natural(self, k):
        return slice(k * self.block, (k + 1) * self.block)

    def blocks(self):
        return range(2 * self.outer)

    def quarter_of(self, d):
        start = (self.rank ^ TURNS[d]) * self.quarter
        return pl.ds(pl.multiple_of(start, self.quarter), self.quarter)


def mixing_forward_kernel(
    order, where, h, w_mix, gain, bias, mixer, streams, normed, coef_out, pre_out
):
    order = order(where)
    hist_len, rows, width = h.shape
    step = 512
    xhat, _ = standardise(h[hist_len - 1].astype(F32))
    mix_normed = (xhat * gain[0:1, :]).astype(BF)
    pre = dot_nt(mix_normed, w_mix[...])
    hidden = gelu_both(pre)[0].astype(BF)
    coef = dot(hidden, mixer[...])
    pre_out[...] = pre
    coef_out[...] = coef
    for start in range(0, width, step):
        lanes = slice(start, start + step)
        parts = [h[j, :, lanes].astype(F32) for j in range(hist_len)]
        for a in range(4):
            first = a * hist_len
            total = coef[:, first : first + 1] * parts[0]
            for j in range(1, hist_len):
                total = total + coef[:, first + j : first + j + 1] * parts[j]
            streams[a, :, lanes] = total
    for a in range(3):
        xhat, _ = standardise(streams[a])
        low = (xhat * gain[1:2, :] + bias[0:1, :]).astype(BF)
        for k in order.blocks():
            normed[a, :, order.relative(k)] = low[:, order.natural(k)]


def turn(values, cos_table, sin_table):
    half_width = ROT // 2
    lane = lax.broadcasted_iota(jnp.int32, values.shape, 1)
    partner = jnp.where(
        lane < half_width,
        pltpu.roll(values, HD - half_width, axis=1),
        pltpu.roll(values, half_width, axis=1),
    )
    return values * cos_table + partner * sin_table


def head_scores(query, key):
    seq_len = query.shape[0]
    scores = dot_nt(query, key) * (1.0 / math.sqrt(HD))
    row = lax.broadcasted_iota(jnp.int32, (seq_len, seq_len), 0)
    column = lax.broadcasted_iota(jnp.int32, (seq_len, seq_len), 1)
    scores = jnp.where(row >= column, scores, NEGATIVE)
    exponent = jnp.exp(scores - jnp.max(scores, axis=-1, keepdims=True))
    return exponent / jnp.sum(exponent, axis=-1, keepdims=True)


def attention_forward_kernel(*refs):
    normed, (own, other, cos, sin) = refs[:4], refs[4:8]
    attended, query_rot, key_rot, value, made, held, arrived = refs[8:]
    quarter = attended.shape[1]
    half = own.shape[0]
    seq_len = cos.shape[0]
    copies = [
        pltpu.make_async_copy(normed[d], held.at[d], arrived.at[d]) for d in range(4)
    ]
    for copy in copies:
        copy.start()
    cos_table, sin_table = cos[...], sin[...]
    for d in range(4):
        copies[d].wait()
        rows = slice(d * seq_len, (d + 1) * seq_len)
        for a in range(3):
            lanes = slice(a * quarter, (a + 1) * quarter)
            made[a] = dot(held[d, a, :, :half], own[:, lanes]) + dot(
                held[d, a, :, half:], other[:, lanes]
            )
        value[rows, :] = made[2].astype(BF)
        for head in range(quarter // HD):
            lanes = slice(head * HD, (head + 1) * HD)
            query = turn(made[0, :, lanes], cos_table, sin_table).astype(BF)
            key = turn(made[1, :, lanes], cos_table, sin_table).astype(BF)
            query_rot[rows, lanes] = query
            key_rot[rows, lanes] = key
            probs = head_scores(query, key).astype(BF)
            attended[rows, lanes] = dot(probs, value[rows, lanes]).astype(BF)


def attention_backward_kernel(q, k, v, g, own, other, cos, sin, grads, *backs):
    quarter = q.shape[1]
    half = own.shape[0]
    scale = 1.0 / math.sqrt(HD)
    cos_table, sin_table = cos[...], -sin[...]
    for head in range(quarter // HD):
        lanes = slice(head * HD, (head + 1) * HD)
        query, key, grad = q[:, lanes], k[:, lanes], g[:, lanes]
        probs = head_scores(query, key)
        grad_probs = dot_nt(grad, v[:, lanes])
        centre = jnp.sum(probs * grad_probs, axis=-1, keepdims=True)
        grad_scores = (probs * (grad_probs - centre)).astype(BF)
        grads[0, :, lanes] = turn(dot(grad_scores, key) * scale, cos_table, sin_table).astype(BF)
        grads[1, :, lanes] = turn(
            dot_tn(grad_scores, query) * scale, cos_table, sin_table
        ).astype(BF)
        grads[2, :, lanes] = dot_tn(probs.astype(BF), grad).astype(BF)

    def send(outs):
        for a in range(3):
            columns = slice(a * quarter, (a + 1) * quarter)
            outs[a][:, :half] = dot_nt(grads[a], own[:, columns]).astype(BF)
            outs[a][:, half:] = dot_nt(grads[a], other[:, columns]).astype(BF)

    for step in range(2):
        outs = backs[3 * step : 3 * step + 3]
        pl.when(pl.program_id(0) == step)(functools.partial(send, outs))


def residual_kernel(order, where, *refs):
    order = order(where)
    parts, weights = refs[:4], refs[4:12]
    stream, gain, bias, residual, normed, attended, natural = refs[12:]
    half = weights[0].shape[0]
    for d in range(4):
        natural[:, order.quarter_of(d)] = parts[d][...]
    for k in order.blocks():
        attended[:, order.relative(k)] = natural[:, order.natural(k)]
    for d in range(4):
        columns = order.quarter_of(d)
        residual[:, columns] = (
            stream[0, :, columns]
            + dot(attended[:, :half], weights[2 * d][...])
            + dot(attended[:, half:], weights[2 * d + 1][...])
        )
    xhat, _ = standardise(residual[...])
    low = (xhat * gain[2:3, :] + bias[1:2, :]).astype(BF)
    for k in order.blocks():
        normed[:, order.relative(k)] = low[:, order.natural(k)]


def up_kernel(*refs):
    rows, (own, other, activated, slope) = refs[:4], refs[4:]
    half = own.shape[0]
    seq_len = rows[0].shape[0]
    for d in range(4):
        up = dot(rows[d][:, :half], own[...]) + dot(rows[d][:, half:], other[...])
        active, back = gelu_both(up)
        activated[d * seq_len : (d + 1) * seq_len, :] = active.astype(BF)
        slope[d * seq_len : (d + 1) * seq_len, :] = back


def down_grad_kernel(activated, *refs):
    rows, out = refs[:4], refs[4]
    seq_len = rows[0].shape[0]
    total = dot_tn(activated[:seq_len, :], rows[0][...])
    for d in range(1, 4):
        total = total + dot_tn(activated[d * seq_len : (d + 1) * seq_len, :], rows[d][...])
    out[...] = total.astype(BF)


def hidden_back_kernel(*refs):
    rows, (weight, slope, out) = refs[:4], refs[4:]
    seq_len = rows[0].shape[0]
    for d in range(4):
        part = slice(d * seq_len, (d + 1) * seq_len)
        out[part, :] = (dot_nt(rows[d][...], weight[...]) * slope[part, :]).astype(BF)


def down_kernel(activated, weight, *outs):
    total = dot(activated[...], weight[...]).astype(BF)
    seq_len = outs[0].shape[0]
    for d in range(4):
        outs[d][...] = total[d * seq_len : (d + 1) * seq_len]


def up_grad_kernel(*refs):
    rows, (grad, out) = refs[:4], refs[4:]
    seq_len = rows[0].shape[0]
    total = dot_tn(rows[0][...], grad[:seq_len, :])
    for d in range(1, 4):
        total = total + dot_tn(rows[d][...], grad[d * seq_len : (d + 1) * seq_len, :])
    out[...] = total.astype(BF)


def normed_back_kernel(pair, grad, own, other, *outs):
    step, steps = pl.program_id(0), pl.num_programs(0)
    seq_len = outs[0].shape[0]

    def send(weight):
        for d, out in zip(pair, outs):
            rows = slice(d * seq_len, (d + 1) * seq_len)
            out[...] = dot_nt(grad[rows, :], weight[...]).astype(BF)

    pl.when(step < steps // 2)(functools.partial(send, own))
    pl.when(step >= steps // 2)(functools.partial(send, other))


def residual_back_kernel(order, where, *refs):
    order = order(where)
    residual, gain, mine, from_core, from_x, grad_out = refs[:6]
    weights = refs[6:14]
    grad, grad_gain, grad_bias = refs[14:17]
    parts, wide, low = refs[17:21], refs[21], refs[22]
    half = weights[0].shape[0]
    for k in order.blocks():
        source = order.relative(k)
        wide[:, order.natural(k)] = (
            mine[:, source].astype(F32)
            + from_core[:, source].astype(F32)
            + from_x[:, source].astype(F32)
        )
    xhat, scale = standardise(residual[...])
    grad_y = wide[...]
    grad_gain[...] = jnp.sum(grad_y * xhat, axis=0, keepdims=True)
    grad_bias[...] = jnp.sum(grad_y, axis=0, keepdims=True)
    grad_x = norm_back(grad_y * gain[2:3, :], xhat, scale)
    grad[...] = (grad_out[...].astype(F32) + grad_x).astype(BF)
    for s in range(2):
        total = dot_nt(grad[:, order.quarter_of(0)], weights[s][...])
        for d in range(1, 4):
            total = total + dot_nt(grad[:, order.quarter_of(d)], weights[2 * d + s][...])
        low[:, s * half : (s + 1) * half] = total.astype(BF)
    for k in order.blocks():
        wide[:, order.natural(k)] = low[:, order.relative(k)].astype(F32)
    for d in range(4):
        parts[d][...] = wide[:, order.quarter_of(d)].astype(BF)


def out_grad_kernel(order, where, attended, grad, *outs):
    order = order(where)
    for d in range(4):
        outs[d][...] = dot_tn(attended[...], grad[:, order.quarter_of(d)]).astype(BF)


def in_grad_kernel(*refs):
    normed, (even, odd, out) = refs[:4], refs[4:]
    seq_len = normed[0].shape[1]
    total = None
    for d in range(4):
        rows = slice(d // 2 * seq_len, (d // 2 + 1) * seq_len)
        part = dot_tn(normed[d][0], (odd if d % 2 else even)[0, rows, :])
        total = part if total is None else total + part
    out[...] = total.astype(BF)


def mixing_backward_kernel(order, where, *refs):
    order = order(where)
    h, streams, coef_in, pre_in = refs[:4]
    mine, from_core, from_x = refs[4:7], refs[7:10], refs[10]
    grad_residual, w_mix, gain, mixer = refs[11:15]
    grad_history, grad_mix, grad_mixer, grad_gains, grad_bias = refs[15:20]
    grad_streams = refs[20]
    hist_len, rows, width = h.shape
    step = 512

    @pl.when(pl.program_id(0) == 0)
    def _():
        grad_mix[...] = jnp.zeros_like(grad_mix)
        grad_mixer[...] = jnp.zeros_like(grad_mixer)
        grad_gains[...] = jnp.zeros_like(grad_gains)
        grad_bias[...] = jnp.zeros_like(grad_bias)

    for a in range(3):
        for k in order.blocks():
            source = order.relative(k)
            grad_streams[a, :, order.natural(k)] = (
                mine[a][:, source].astype(F32)
                + from_core[a][:, source].astype(F32)
                + from_x[a, :, source].astype(F32)
            )
        xhat, scale = standardise(streams[a])
        grad_y = grad_streams[a]
        grad_gains[1:2, :] += jnp.sum(grad_y * xhat, axis=0, keepdims=True)
        grad_bias[...] += jnp.sum(grad_y, axis=0, keepdims=True)
        grad_streams[a] = norm_back(grad_y * gain[1:2, :], xhat, scale)
    grad_streams[3] = grad_residual[...].astype(F32)

    coef = coef_in[...]
    columns = coef.shape[1]
    sums = [jnp.zeros((rows, 128), F32) for _ in range(columns)]
    for start in range(0, width, step):
        lanes = slice(start, start + step)
        grads = [grad_streams[a, :, lanes] for a in range(4)]
        for j in range(hist_len):
            part = h[j, :, lanes].astype(F32)
            back = coef[:, j : j + 1] * grads[0]
            for a in range(1, 4):
                at = a * hist_len + j
                back = back + coef[:, at : at + 1] * grads[a]
            for a in range(4):
                product = grads[a] * part
                folded = product[:, 0:128]
                for lane in range(128, step, 128):
                    folded = folded + product[:, lane : lane + 128]
                sums[a * hist_len + j] = sums[a * hist_len + j] + folded
            if j < hist_len - 1:
                grad_history[j, :, lanes] = back.astype(BF)
            else:
                grad_streams[3, :, lanes] = back
    lane = lax.broadcasted_iota(jnp.int32, (rows, columns), 1)
    grad_coef = jnp.zeros((rows, columns), F32)
    for at in range(columns):
        grad_coef = jnp.where(lane == at, jnp.sum(sums[at], axis=-1, keepdims=True), grad_coef)
    grad_coef = grad_coef.astype(BF)
    hidden, slope = gelu_both(pre_in[...])
    hidden = hidden.astype(BF)
    grad_mixer[...] += dot_tn(hidden, grad_coef)
    grad_pre = (dot_nt(grad_coef, mixer[...]) * slope).astype(BF)
    xhat, scale = standardise(h[hist_len - 1].astype(F32))
    grad_mix[...] += dot_tn(grad_pre, (xhat * gain[0:1, :]).astype(BF))
    grad_y = dot(grad_pre, w_mix[...])
    grad_gains[0:1, :] += jnp.sum(grad_y * xhat, axis=0, keepdims=True)
    grad_current = norm_back(grad_y * gain[0:1, :], xhat, scale)
    grad_history[hist_len - 1] = (grad_streams[3] + grad_current).astype(BF)


def rotary_tables(seq_len):
    half_width = ROT // 2
    frequency = 10000.0 ** (-(2.0 * jnp.arange(half_width, dtype=F32)) / ROT)
    angles = jnp.arange(seq_len, dtype=F32)[:, None] * frequency[None, :]
    cosine, sine = jnp.cos(angles), jnp.sin(angles)
    rest = HD - ROT
    cos_table = jnp.concatenate([cosine, cosine, jnp.ones((seq_len, rest), F32)], axis=1)
    sin_table = jnp.concatenate([-sine, sine, jnp.zeros((seq_len, rest), F32)], axis=1)
    return cos_table, sin_table


def place_kernel(order, where, *refs):
    order = order(where)
    parts, (weight_in, weight_out) = refs[:4], refs[4:]
    quarter = order.quarter
    for d in range(4):
        for a in range(4):
            start = (a % 3) * 4 * quarter + (order.rank ^ TURNS[d]) * quarter
            lanes = pl.ds(pl.multiple_of(start, quarter), quarter)
            target = weight_out if a == 3 else weight_in
            if a == 3:
                lanes = order.quarter_of(d)
            target[:, lanes] = parts[d][:, a * quarter : (a + 1) * quarter]


def moments_kernel(share, clip_ref, *refs):
    clip = clip_ref[0]
    step = 512

    @pl.when(pl.program_id(0) == 0)
    def _():
        for member in range(4):
            refs[26][member] = 0.0
        refs[26][4] = jnp.sum(refs[16][...] * refs[16][...])
        refs[26][5] = jnp.sum(refs[17][...] * refs[17][...]) * share

    for member in range(4):
        grad, first, second, weight = refs[4 * member : 4 * member + 4]
        first_out, second_out = refs[18 + 2 * member : 20 + 2 * member]
        total = 0.0
        for start in range(0, grad.shape[1], step):
            lanes = slice(start, start + step)
            scaled = grad[:, lanes].astype(F32) * clip
            first_new = BETA * first[:, lanes] + (1.0 - BETA) * scaled
            second_new = BETA * second[:, lanes] + (1.0 - BETA) * scaled * scaled
            first_out[:, lanes] = first_new
            second_out[:, lanes] = second_new
            change = first_new / (jnp.sqrt(second_new) + EPS_ADAM) + DECAY_WEIGHT * weight[:, lanes]
            total = total + jnp.sum(change * change, axis=0, keepdims=True)
        refs[26][member] = refs[26][member] + jnp.sum(total)


def apply_kernel(trust_ref, *refs):
    step = 512
    for member in range(4):
        first, second, weight = refs[3 * member : 3 * member + 3]
        out, low = refs[20 + 2 * member : 22 + 2 * member]
        rate = RATE_MATRIX * trust_ref[member]
        for start in range(0, weight.shape[1], step):
            lanes = slice(start, start + step)
            old = weight[:, lanes]
            change = first[:, lanes] / (jnp.sqrt(second[:, lanes]) + EPS_ADAM) + DECAY_WEIGHT * old
            new = old - rate * change
            out[:, lanes] = new
            low[:, lanes] = new.astype(BF)

    @pl.when(pl.program_id(0) == 0)
    def _():
        for member in range(4):
            change, weight = refs[12 + 2 * member : 14 + 2 * member]
            out, low = refs[28 + 2 * member : 30 + 2 * member]
            rate = RATE_MATRIX * trust_ref[4 + member] if member < 2 else RATE_VECTOR
            new = weight[...] - rate * change[...]
            out[...] = new
            low[...] = new.astype(BF)


class Links:
    def __init__(self, devices, width):
        self.devices = devices
        index = lax.axis_index("dp")
        self.core = index & 1
        self.x = (index >> 1) & 1
        self.rank = index & 3
        self.index = index
        self.y_bit = 2
        self.block = 4 * width // devices
        while self.block % 128:
            self.y_bit += 1
            self.block *= 2
        self.inner = 1 << (self.y_bit - 2)
        self.outer = width // (2 * self.block)
        self.y = (index >> self.y_bit) & 1
        self.where = jnp.stack([self.rank, self.y]).astype(jnp.int32)
        groups = {}
        for j in range(devices):
            groups.setdefault((j & 3, (j >> self.y_bit) & 1), []).append(j)
        self.z_groups = list(groups.values())

    def swap(self, value, bit):
        return lax.ppermute(value, "dp", [(j, j ^ bit) for j in range(self.devices)])

    def swap_core(self, value):
        return self.swap(value, 1)

    def swap_x(self, value):
        return self.swap(value, 2)

    def swap_y(self, value):
        return self.swap(value, 1 << self.y_bit)

    def gather(self, value, groups):
        return lax.all_gather(value, "dp", axis=0, tiled=True, axis_index_groups=groups)

    def reduce(self, value, groups):
        return lax.psum_scatter(
            value, "dp", scatter_dimension=0, tiled=True, axis_index_groups=groups
        )

    def total(self, value):
        bit = 1
        while bit < self.devices:
            pair = value + self.swap(value, bit)
            if 2 * bit < self.devices:
                pair = pair + (self.swap(value, 2 * bit) + self.swap(value, 3 * bit))
            value = pair
            bit *= 4
        return value

    def to_absolute(self, parts):
        own, across_x, across_core, across_both = parts
        low_x = self.x == 0
        core_own = (jnp.where(low_x, own, across_x), jnp.where(low_x, across_x, own))
        core_other = (
            jnp.where(low_x, across_core, across_both),
            jnp.where(low_x, across_both, across_core),
        )
        low_core = self.core == 0
        ordered = []
        for mine, other in zip(core_own, core_other):
            ordered.append(jnp.where(low_core, mine, other))
            ordered.append(jnp.where(low_core, other, mine))
        return ordered

    def to_relative(self, parts):
        low_x, low_core = self.x == 0, self.core == 0
        near = [jnp.where(low_x, parts[c], parts[2 + c]) for c in (0, 1)]
        far = [jnp.where(low_x, parts[2 + c], parts[c]) for c in (0, 1)]
        return [
            jnp.where(low_core, near[0], near[1]),
            jnp.where(low_core, far[0], far[1]),
            jnp.where(low_core, near[1], near[0]),
            jnp.where(low_core, far[1], far[0]),
        ]

    def group_gather(self, value):
        across_x = self.swap_x(value)
        return [value, across_x, self.swap_core(value), self.swap_core(across_x)]

    def group_exchange(self, parts):
        own, *others = parts
        return [own] + [self.swap(part, turn) for part, turn in zip(others, TURNS[1:])]

    def group_reduce(self, own, for_x, for_core, for_both, *ties):
        from_both = self.swap_core(for_both)
        for_x = (for_x.astype(F32) + from_both.astype(F32)).astype(BF)
        return self.swap_core(for_core), self.swap_x(after(for_x, *ties)), for_x


def program(
    devices,
    history,
    d_out,
    group_ids,
    group_weight,
    attn_in,
    attn_out,
    ffn_up,
    ffn_down,
    mixer_in,
    mixer_out,
    norm_gain,
    norm_bias,
    first_attn_in,
    second_attn_in,
    first_attn_out,
    second_attn_out,
    first_ffn_up,
    second_ffn_up,
    first_ffn_down,
    second_ffn_down,
    first_mixer_in,
    second_mixer_in,
    first_mixer_out,
    second_mixer_out,
    first_norm_gain,
    second_norm_gain,
    first_norm_bias,
    second_norm_bias,
):
    hist_len, seq_len, width = history.shape
    links = Links(devices, width)
    order = functools.partial(
        Order, outer=links.outer, block=links.block, quarter=width // 4
    )
    with_order = lambda kernel: functools.partial(kernel, order)
    where = (links.where, SMEM)
    quarter, half = width // 4, width // 2
    rows = width // devices
    hidden = ffn_down.shape[0] * devices
    units = hidden // devices
    share = hidden // 4
    four = 4 * seq_len
    whole = lambda array: (array, fixed(array))

    low_attn = attn_in.astype(BF).reshape(rows, 3, 4, quarter)
    low_out = attn_out.astype(BF).reshape(rows, 1, 4, quarter)
    by_rank = jnp.concatenate([low_attn, low_out], axis=1)
    by_rank = [by_rank[:, :, r].reshape(rows, width) for r in range(4)]
    attn_parts = links.group_exchange(links.to_relative(by_rank))
    attn_block = jnp.concatenate(links.to_absolute(attn_parts), axis=0)

    low_up = ffn_up.astype(BF).reshape(rows, links.outer, 2, links.inner, 4, units)
    low_up = jnp.transpose(low_up, (4, 0, 1, 3, 2, 5)).reshape(4, rows, share)
    up_parts = after(links.to_relative(list(low_up)), attn_parts[1], attn_parts[3])
    up_parts = links.group_exchange(up_parts)
    up_block = jnp.concatenate(links.to_absolute(up_parts), axis=0)

    low_down = ffn_down.astype(BF)
    other_down = links.swap_y(low_down)
    low_y = links.y == 0

    attn_own = links.gather(attn_block, links.z_groups)
    attn_other = links.swap_y(attn_own)
    up_own = links.gather(up_block, links.z_groups)
    up_other = links.swap_y(up_own)

    hidden_mix = mixer_in.shape[1]
    pack = jnp.concatenate([mixer_in.T, norm_gain, norm_bias], axis=0).astype(BF)
    bit = 1
    while bit < devices:
        other = links.swap(pack, bit)
        low = (links.index & bit) == 0
        pack = jnp.concatenate([jnp.where(low, pack, other), jnp.where(low, other, pack)], axis=1)
        bit *= 2
    w_mixer_in = pack[:hidden_mix]
    gain_table = pack[hidden_mix : hidden_mix + 3].astype(F32)
    bias_table = pack[hidden_mix + 3 :].astype(F32)
    mixer_low = mixer_out.astype(BF)

    tile = 64
    steps = (seq_len // tile,)
    columns = mixer_out.shape[1]
    row_tile = lambda *lead: pl.BlockSpec(
        lead + (tile, width), lambda t: (0,) * len(lead) + (t, 0)
    )
    narrow = pl.BlockSpec((tile, columns), lambda t: (t, 0))
    pre_narrow = pl.BlockSpec((tile, hidden_mix), lambda t: (t, 0))
    streams, normed, coef, mix_pre = run(
        with_order(mixing_forward_kernel),
        14,
        steps,
        [
            where,
            (history, row_tile(hist_len)),
            whole(w_mixer_in),
            whole(gain_table),
            whole(bias_table),
            whole(mixer_low),
        ],
        [
            ((4, seq_len, width), F32, row_tile(4)),
            ((3, seq_len, width), BF, row_tile(3)),
            ((seq_len, columns), F32, narrow),
            ((seq_len, hidden_mix), F32, pre_narrow),
        ],
    )

    low_down, other_down = after((low_down, other_down), normed)
    down_block = jnp.concatenate(
        [jnp.where(low_y, low_down, other_down), jnp.where(low_y, other_down, low_down)], axis=0
    )
    w_down = links.gather(down_block, links.z_groups)

    tables = [whole(table) for table in rotary_tables(seq_len)]
    normed_four = links.group_gather(normed)
    attn_weights = [
        (
            array,
            pl.BlockSpec((half, 3 * quarter), lambda s: (0, 0), pipeline_mode=pl.Buffered(1)),
        )
        for array in (attn_own, attn_other)
    ]
    out_mine = [array[:, 3 * quarter :] for array in (attn_own, attn_other)]
    out_x = [links.swap_x(array) for array in out_mine]
    group_count = group_weight.shape[0]
    seq_weight = jnp.sum(
        jnp.where(jnp.arange(group_count, dtype=jnp.int32) == group_ids[0], group_weight, 0.0)
    )
    grad_out = (d_out.astype(F32) * seq_weight).astype(BF)
    grad_out = after(grad_out, normed_four[1])
    grad_out_x = links.swap_x(grad_out)
    seq_block = pl.BlockSpec((seq_len, quarter), lambda s: (s, 0))
    attn_other_now = after(attn_other, grad_out_x)
    anywhere = pl.BlockSpec(memory_space=pl.ANY)
    four_quarter = pl.BlockSpec((four, quarter), lambda _: (0, 0))
    attended, query_rot, key_rot, value = run(
        attention_forward_kernel,
        16,
        (1,),
        [(part, anywhere) for part in normed_four]
        + [(attn_own, attn_weights[0][1]), (attn_other_now, attn_weights[0][1])]
        + tables,
        [((four, quarter), BF, four_quarter)] * 4,
        [
            pltpu.VMEM((3, seq_len, quarter), F32),
            pltpu.VMEM((4, 3, seq_len, width), BF),
            pltpu.SemaphoreType.DMA((4,)),
        ],
    )
    out_x = after(out_x, attended)
    out_halves = [
        [out_mine[k], out_x[k], links.swap_core(out_mine[k]), links.swap_core(out_x[k])]
        for k in range(2)
    ]
    w_out = [out_halves[k][d] for d in range(4) for k in range(2)]
    attended = links.group_exchange(
        [attended[d * seq_len : (d + 1) * seq_len] for d in range(4)]
    )
    one_row = ((1, width), F32, pl.BlockSpec((1, width), lambda *_: (0, 0)))
    full = lambda kind: (
        (seq_len, width),
        kind,
        pl.BlockSpec((seq_len, width), lambda *_: (0, 0)),
    )
    residual, ffn_normed, attended_rel = run(
        with_order(residual_kernel),
        9,
        (1,),
        [where]
        + [whole(part) for part in attended]
        + [whole(part) for part in w_out]
        + [
            (
                streams,
                pl.BlockSpec(
                    (1, seq_len, width), lambda _: (3, 0, 0), pipeline_mode=pl.Buffered(1)
                ),
            ),
            whole(gain_table),
            whole(bias_table),
        ],
        [full(F32), full(BF), full(BF)],
        [pltpu.VMEM((seq_len, width), BF)],
    )

    ffn_four = links.group_gather(ffn_normed)
    wide = 256
    column_tile = lambda count: pl.BlockSpec((count, wide), lambda t: (0, t))
    line_tile = lambda count: pl.BlockSpec((wide, count), lambda t: (t, 0))
    activated, slope = run(
        up_kernel,
        17,
        (share // wide,),
        [whole(part) for part in ffn_four]
        + [(up_own, column_tile(half)), (up_other, column_tile(half))],
        [((four, share), BF, column_tile(four)), ((four, share), F32, column_tile(four))],
    )

    grad_out_x = after(grad_out_x, activated)
    grad_out_four = [
        grad_out,
        grad_out_x,
        links.swap_core(grad_out),
        links.swap_core(grad_out_x),
    ]

    (grad_down,) = run(
        down_grad_kernel,
        14,
        (share // wide,),
        [(activated, column_tile(four))] + [whole(part) for part in grad_out_four],
        [((share, width), BF, line_tile(width))],
    )
    down_sums = links.reduce(grad_down, links.z_groups)

    (grad_up,) = run(
        hidden_back_kernel,
        16,
        (share // wide,),
        [whole(part) for part in grad_out_four]
        + [(w_down, line_tile(width)), (after(slope, grad_down), column_tile(four))],
        [((four, share), BF, column_tile(four))],
    )

    def rows_of_four(block):
        parts = list(block.reshape(4, rows, block.shape[1]))
        return links.group_exchange(links.to_relative(parts))

    def whole_rows(parts):
        return jnp.stack(links.to_absolute(parts), axis=1)

    tiles = half // wide

    def normed_back(pair, grad):
        return run(
            functools.partial(normed_back_kernel, pair),
            11,
            (2 * tiles,),
            [
                whole(grad),
                (up_own, pl.BlockSpec((wide, share), lambda t: (jnp.minimum(t, tiles - 1), 0))),
                (up_other, pl.BlockSpec((wide, share), lambda t: (jnp.maximum(t - tiles, 0), 0))),
            ],
            [((seq_len, width), BF, column_tile(seq_len))] * 2,
        )

    def up_grad(first, count, grad):
        block = pl.BlockSpec((seq_len, wide), lambda t: (0, first + t))
        (out,) = run(
            up_grad_kernel,
            9,
            (count,),
            [(part, block) for part in ffn_four] + [whole(grad)],
            [((count * wide, share), BF, line_tile(share))],
        )
        return out

    for_x, for_both = normed_back((1, 3), grad_up)
    up_first = up_grad(tiles, 1, after(grad_up, for_both))
    up_theirs_first = links.swap_y(up_first)
    up_second = up_grad(tiles + 1, 1, after(grad_up, up_first))
    up_theirs_second = links.swap_y(up_second)
    up_rest = up_grad(tiles + 2, tiles - 2, after(grad_up, up_second))
    up_theirs_rest = links.swap_y(up_rest)
    own, for_core = normed_back((0, 2), after(grad_up, up_rest))
    up_grad_own = up_grad(0, tiles, after(grad_up, own))
    from_core, from_x, _ = links.group_reduce(own, for_x, for_core, for_both)
    from_x = after(from_x, up_grad_own, up_theirs_first)
    part_out = ((seq_len, quarter), BF, pl.BlockSpec((seq_len, quarter), lambda _: (0, 0)))
    back = run(
        with_order(residual_back_kernel),
        11,
        (1,),
        [
            where,
            whole(residual),
            whole(gain_table),
            whole(own),
            whole(from_core),
            whole(from_x),
            whole(grad_out),
        ]
        + [whole(part) for part in w_out],
        [full(BF), one_row, one_row] + [part_out] * 4,
        [pltpu.VMEM((seq_len, width), F32), pltpu.VMEM((seq_len, width), BF)],
    )
    grad_residual, grad_gain_ffn, grad_bias_ffn = back[:3]

    grad_heads = links.group_exchange(back[3:])

    line = 512
    out_parts = run(
        with_order(out_grad_kernel),
        7,
        (width // line,),
        [
            where,
            (attended_rel, pl.BlockSpec((seq_len, line), lambda t: (0, t))),
            whole(grad_residual),
        ],
        [((width, quarter), BF, pl.BlockSpec((line, quarter), lambda t: (t, 0)))] * 4,
    )
    out_parts = after(out_parts, grad_heads[1], grad_heads[3])
    out_both = [links.swap_core(out_parts[3][k * half : (k + 1) * half]) for k in range(2)]
    out_core = links.swap_core(out_parts[2])

    def attention_back(first, *ties):
        heads = jnp.concatenate([grad_heads[first], grad_heads[first + 2]], axis=0)
        block = pl.BlockSpec((seq_len, quarter), lambda s: (first + 2 * s, 0))
        proj, *backs = run(
            attention_backward_kernel,
            15,
            (2,),
            [(query_rot, block), (key_rot, block), (value, block)]
            + [(after(heads, *ties), seq_block)]
            + attn_weights
            + tables,
            [
                (
                    (3, 2 * seq_len, quarter),
                    BF,
                    pl.BlockSpec((3, seq_len, quarter), lambda s: (0, s, 0)),
                )
            ]
            + [full(BF)] * 6,
        )
        return proj, backs[:3], backs[3:]

    plus = lambda mine, theirs: (mine.astype(F32) + theirs.astype(F32)).astype(BF)
    proj_odd, for_x, for_both = attention_back(1, up_theirs_second)
    out_both = after(out_both, for_both)
    out_for_x = [plus(out_parts[1][k * half : (k + 1) * half], out_both[k]) for k in range(2)]
    out_x_other = links.swap_x(out_for_x[1])
    out_x_own = links.swap_x(out_for_x[0])
    proj_even, own, for_core = attention_back(0, out_for_x)
    back_own = own
    from_both = [links.swap_core(part) for part in for_both]
    back_core = [links.swap_core(part) for part in for_core]
    for_x = jnp.stack([plus(part, other) for part, other in zip(for_x, from_both)])
    back_x = links.swap_x(for_x)
    proj_even = after(proj_even, for_x)

    def in_grad(s, proj):
        block = pl.BlockSpec((1, seq_len, wide), lambda a, t: (a, 0, s * tiles + t))
        proj_block = pl.BlockSpec((1, 2 * seq_len, quarter), lambda a, t: (a, 0, 0))
        (out,) = run(
            in_grad_kernel,
            12,
            (3, tiles),
            [(part, block) for part in normed_four] + [(proj, proj_block), (proj_odd, proj_block)],
            [((half, 3 * quarter), BF, pl.BlockSpec((wide, quarter), lambda a, t: (t, a)))],
        )
        return out

    in_grad_other = in_grad(1, proj_even)
    in_theirs = links.swap_y(in_grad_other)
    in_grad_own = in_grad(0, after(proj_even, in_grad_other))

    up_theirs = jnp.concatenate(
        [up_theirs_first, up_theirs_second, after(up_theirs_rest, in_grad_own, out_x_other)]
    )
    up_both = after(plus(up_grad_own, up_theirs), down_sums)
    up_sums = links.reduce(up_both, links.z_groups)
    three = lambda k, theirs: (
        out_parts[0][k * half : (k + 1) * half].astype(F32)
        + out_core[k * half : (k + 1) * half].astype(F32)
        + theirs.astype(F32)
    )
    out_theirs = links.swap_y(three(1, after(out_x_other, up_both)).astype(BF))

    down_parts = run(
        down_kernel,
        14,
        (width // wide,),
        [whole(after(activated, up_both)), (w_down, column_tile(share))],
        [((seq_len, width), BF, column_tile(seq_len))] * 4,
    )
    down_core = links.swap_core(down_parts[2])
    down_for_x = plus(down_parts[1], links.swap_core(down_parts[3]))

    weights = (attn_in, attn_out, ffn_up, ffn_down, mixer_in, mixer_out, norm_gain, norm_bias)
    square = lambda array: jnp.sum(jnp.square(array.astype(F32)))

    def portion(member, amount):
        return amount / devices if member == 5 else amount


    in_theirs = after(in_theirs, down_for_x)
    attn_both = jnp.concatenate(
        [plus(in_grad_own, in_theirs), plus(three(0, out_x_own), out_theirs)], axis=1
    )
    attn_both = after(attn_both, up_sums, back_x, back_core)
    up_four = rows_of_four(after(up_sums, attn_both))
    attn_sums = links.reduce(attn_both, links.z_groups)


    fixed_out = lambda shape: (
        shape,
        F32,
        pl.BlockSpec(shape, lambda t: (0, 0)),
    )
    grad_history, grad_mixer_in, grad_mixer_out, grad_gains, grad_bias_attn = run(
        with_order(mixing_backward_kernel),
        450,
        steps,
        [
            where,
            (history, row_tile(hist_len)),
            (streams, row_tile(3)),
            (coef, narrow),
            (mix_pre, pre_narrow),
        ]
        + [(part, row_tile()) for part in (*back_own, *back_core)]
        + [
            (back_x, row_tile(3)),
            (after(grad_residual, attn_both), row_tile()),
            whole(w_mixer_in),
            whole(gain_table),
            whole(mixer_low),
        ],
        [
            ((hist_len, seq_len, width), BF, row_tile(hist_len)),
            fixed_out((hidden_mix, width)),
            fixed_out((hidden_mix, columns)),
            fixed_out((2, width)),
            fixed_out((1, width)),
        ],
        [pltpu.VMEM((4, tile, width), F32)],
    )

    shard_up = jnp.transpose(
        whole_rows(up_four).reshape(rows, 4, links.outer, links.inner, 2, units),
        (0, 2, 4, 3, 1, 5),
    ).reshape(rows, hidden)

    down_x = links.swap_x(after(down_for_x, grad_gains))
    small = jnp.concatenate(
        [grad_mixer_in, grad_gains, grad_gain_ffn, grad_bias_attn, grad_bias_ffn], axis=0
    )
    down_sums = after(down_sums, attn_both)
    down_sums = down_sums.reshape(2, units, width)
    down_mine = jnp.where(low_y, down_sums[0], down_sums[1])
    down_theirs = jnp.where(low_y, down_sums[1], down_sums[0])
    down_theirs = links.swap_y(down_theirs)
    shard_down = down_mine.astype(F32) + down_theirs.astype(F32)
    small = after(small, down_theirs)
    top = devices.bit_length() - 2
    inner = 1 << (links.y_bit - 2)
    pieces = small.reshape(small.shape[0], devices // (8 * inner), 2, inner * 4 * rows)
    take = lambda array, at, axis: lax.dynamic_index_in_dim(array, at, axis, keepdims=False)
    pieces = take(pieces, links.y, 2) + links.swap_y(take(pieces, 1 - links.y, 2))
    bits = [k for k in range(top, 1, -1) if k != links.y_bit]
    while bits:
        pair, bits = bits[:2], bits[2:]
        pieces = pieces.reshape(small.shape[0], 1 << len(pair), -1)
        at = sum(((links.index >> k) & 1) << e for e, k in enumerate(reversed(pair)))
        total = take(pieces, at, 1)
        for turn in range(1, 1 << len(pair)):
            mask = sum(((turn >> e) & 1) << k for e, k in enumerate(reversed(pair)))
            total = total + links.swap(take(pieces, at ^ turn, 1), mask)
        pieces = total
    pieces = pieces.reshape(small.shape[0], 4, rows)
    small = take(pieces, links.rank, 1)
    for turn in TURNS[1:]:
        small = small + links.swap(take(pieces, links.rank ^ turn, 1), turn)
    mixer_grad = links.total(grad_mixer_out)
    early_squares = square(up_sums) + square(shard_down) + square(small)
    early_squares = early_squares + square(mixer_grad) / devices
    attn_sums = after(attn_sums, shard_up, shard_down)
    block_of = lambda array_shape: pl.BlockSpec(array_shape, lambda t: (0, 0))
    shard_in, shard_out = run(
        with_order(place_kernel),
        PLACE_COST,
        (1,),
        [where] + [whole(part) for part in rows_of_four(attn_sums)],
        [
            ((rows, 3 * width), BF, block_of((rows, 3 * width))),
            ((rows, width), BF, block_of((rows, width))),
        ],
    )

    grads = (
        shard_in,
        shard_out,
        shard_up,
        shard_down,
        small[:hidden_mix].T,
        mixer_grad,
        small[hidden_mix : hidden_mix + 3],
        small[hidden_mix + 3 :],
    )

    firsts = (
        first_attn_in,
        first_attn_out,
        first_ffn_up,
        first_ffn_down,
        first_mixer_in,
        first_mixer_out,
        first_norm_gain,
        first_norm_bias,
    )
    seconds = (
        second_attn_in,
        second_attn_out,
        second_ffn_up,
        second_ffn_down,
        second_mixer_in,
        second_mixer_out,
        second_norm_gain,
        second_norm_bias,
    )

    local_squares = early_squares + square(attn_sums)
    weights_later = after(weights, coef)
    local_weight_sq = [portion(member, square(weights_later[member])) for member in range(6)]
    sums = links.total(jnp.stack([local_squares] + local_weight_sq))
    squares, weight_sq = sums[0], sums[1:]
    global_norm = jnp.sqrt(squares)
    clip = 0.3 * math.sqrt(PARAMS) / (global_norm + 1e-06)
    parts = rows // 16
    slab = lambda array: pl.BlockSpec(
        (array.shape[0] // parts, array.shape[1]), lambda t: (t, 0)
    )
    slabs = lambda *arrays: [(array, slab(array)) for array in arrays]
    made = lambda array, kind: (array.shape, kind, slab(array))
    ins, outs = [(clip[None], SMEM)], []
    for member in range(4):
        ins += slabs(grads[member], firsts[member], seconds[member], weights[member])
        outs += [made(weights[member], F32)] * 2
    outs.append(((6,), F32, SMEM))
    small_new, steps_small = [], []
    for member in range(4, 8):
        scaled = grads[member] * clip
        first_new = BETA * firsts[member] + (1.0 - BETA) * scaled
        second_new = BETA * seconds[member] + (1.0 - BETA) * scaled * scaled
        step_value = first_new / (jnp.sqrt(second_new) + EPS_ADAM)
        if member < 6:
            step_value = step_value + DECAY_WEIGHT * weights[member]
        small_new.append((first_new, second_new))
        steps_small.append(step_value)
    ins += [whole(steps_small[0]), whole(steps_small[1])]
    moments = run(
        functools.partial(moments_kernel, 1.0 / devices), 14, (parts,), ins, outs
    )
    down_x = after(down_x, moments[8])
    out_state = (
        residual + down_parts[0].astype(F32) + down_core.astype(F32) + down_x.astype(F32)
    ).astype(BF)

    firsts_new = list(moments[0:8:2]) + [first for first, _ in small_new]
    seconds_new = list(moments[1:8:2]) + [second for _, second in small_new]
    update_sq = links.total(moments[8])
    weight_norm = jnp.sqrt(weight_sq)
    update_norm = jnp.sqrt(update_sq)
    trust = weight_norm / (update_norm + 1e-06)
    lamb_stats = jnp.stack([weight_norm, update_norm, trust], axis=1)
    ins, outs = [(trust, SMEM)], []
    for member in range(4):
        ins += slabs(firsts_new[member], seconds_new[member], weights[member])
        outs += [made(weights[member], F32), made(weights[member], BF)]
    for member in range(4, 8):
        shape = weights[member].shape
        spec = pl.BlockSpec(shape, lambda t: (0, 0))
        ins += [(steps_small[member - 4], spec), (weights[member], spec)]
        outs += [(shape, F32, spec), (shape, BF, spec)]
    applied = run(apply_kernel, 10, (parts,), ins, outs)
    results = []
    for member in range(8):
        results += [*applied[2 * member : 2 * member + 2], firsts_new[member], seconds_new[member]]
    return (out_state, grad_history, global_norm, lamb_stats, *results)


def solution(mesh):
    rows, columns, whole = P("dp", None), P(None, "dp"), P()
    middle = P(None, "dp", None)
    matrices = (rows,) * 5 + (whole,) + (columns,) * 2
    moments = tuple(spec for spec in matrices for _ in range(2))
    results = tuple(spec for spec in matrices for _ in range(4))
    return jax.shard_map(
        functools.partial(program, mesh.shape["dp"]),
        mesh=mesh,
        in_specs=(middle, rows, P("dp"), whole) + matrices + moments,
        out_specs=(rows, middle, whole, whole) + results,
        check_vma=False,
    )
```
